32 devices in a mesh: ty: 8 (over y, x, core), tx: 4 (over z).
Axes of the slice: x: 2, y: 2, z: 4, core: 2. Of those that a mesh axis runs over, the one named last changes fastest.
Arguments:
- object_field: float32 [2, 4096, 2048], P(None, 'ty', 'tx'), may hold values from -5 to 5
- probe_field: float32 [2, 128, 128], replicated, may hold values from -5 to 5
- owners: int32 [2, 768, 1], P(None, ('ty', 'tx')), may hold values from 0 to 7; in each aligned block of 24 rows (0 to 23, 24 to 47, ..., all dimensions but the last counted through in order) at most 3 rows name the same one
- row_offsets: int32 [2, 768], P(None, ('ty', 'tx')), may hold values from 0 to 511
- col_offsets: int32 [2, 768], P(None, ('ty', 'tx')), may hold values from 0 to 511
- intensities: float32 [2, 768, 128, 128], P(None, ('ty', 'tx')), may hold values from 0.1 to 3
Outputs:
- new_object: float32 [2, 4096, 2048], P(None, 'ty', 'tx')
- new_probe: float32 [2, 128, 128], replicated
The draws below stay inside these ranges and needn't reach their ends.
Inputs may be any that keep to these rules, and one draw needn't show every extreme that they name: `owners`: in each step the 24 positions of one device name each band at most 3 times; some device names some band exactly 3 times.
All inputs are finite; a program needn't handle non-finite values.
Results may differ from the reference program's by a relative error of at most 0.00022.
Values sent between devices are 32-bit elements; how exact they have to be, the bound alone decides.
A program may use at most 128 MiB of HBM per device.

```python
import math
import jax
import jax.numpy as jnp
import numpy as np
from jax import lax

PATCH = 128
TR = 512
TC = 512
BATCH = 24
CAP = 3
STEPS = 2
BANDS = 8
STRIPS = 4
NR = 4096
NC = 2048
POSITIONS = 768


def place_ends(result, rng, low, largest):
    longest = result.shape.index(max(result.shape))
    spots = []
    for shift in (0, 1):
        where = [jax.random.randint(jax.random.fold_in(rng, axis), (), 0, length) for axis, length in enumerate(result.shape)]
        where[longest] = (where[longest] + shift) % result.shape[longest]
        spots.append(tuple(where))
    return result.at[spots[0]].set(low).at[spots[1]].set(largest)


def level_of(own_key, extent, cuts, smallest, largest):
    level, own = 1.0, jax.random.fold_in(own_key, 6)
    for axis_at, parts in cuts:
        steps = jnp.exp(jax.random.uniform(jax.random.fold_in(own, axis_at), (parts,), jnp.float32, smallest / len(cuts), largest / len(cuts)))
        level = level * jnp.repeat(steps, extent[axis_at] // parts).reshape([-1 if axis == axis_at else 1 for axis in range(len(extent))])
    return level


def routed_block(own_key, own, number, rows, count, top, limit, slope):
    ranking = jax.random.permutation(own_key, count)
    heavy_load, ordinary = portions_of(count, rows * top, limit, slope, True), portions_of(count, rows * top, limit, slope, False)
    places = jnp.arange(count)

    def named(tallies, offset_by):
        used = int((tallies > 0).sum())
        fixed = max(1, used // 4)
        shifted = fixed + (places - fixed + offset_by * (used - fixed)) % max(1, count - fixed)
        return jnp.zeros((count,), jnp.int32).at[ranking[jnp.where(places < fixed, places, shifted)]].set(jnp.asarray(tallies, jnp.int32))

    tallies = jnp.where(number % 4 == 0, named(heavy_load, number // 4), named(ordinary, number - number // 4 - 1))
    mixed = jax.random.permutation(jax.random.fold_in(own, 3), count)
    giver, receiver = mixed[0:count // 2 * 2:2], mixed[1:count // 2 * 2:2]
    slack = jnp.minimum(tallies[giver] - 1, limit - tallies[receiver]) // 2
    slack = jnp.where((giver == ranking[0]) | (receiver == ranking[0]) | (tallies[receiver] == 0), 0, jnp.maximum(slack, 0))
    shifted = jax.random.randint(jax.random.fold_in(own, 4), (count // 2,), 0, 1 << 20) % (slack + 1)
    tallies = tallies.at[giver].add(-shifted).at[receiver].add(shifted)
    members = jnp.searchsorted(jnp.cumsum(tallies), jnp.arange(rows * top), side="right").astype(jnp.int32)
    listing = members.reshape(top, rows).T
    listing = listing[jax.random.permutation(jax.random.fold_in(own, 1), rows)]
    offset_by = jax.random.randint(jax.random.fold_in(own, 2), (rows, 1), 0, top)
    return jnp.take_along_axis(listing, (jnp.arange(top)[None, :] + offset_by) % top, axis=1)


def portions_of(count, total, most, skew, full):
    portions = [(1 << 20) // math.isqrt(rank ** skew) + 1 for rank in range(1, count + 1)]
    largest = most if full else min(most, max(-(-total // count), total * portions[0] // sum(portions)))
    least = 1 if total - largest >= count - 1 else 0
    counts, spare = [largest] + [least] * (count - 1), total - largest - least * (count - 1)
    while spare > 0:
        movable = [i for i in range(1, count) if counts[i] < largest] or [i for i in range(1, count) if counts[i] < most]
        whole, left = sum([portions[i] for i in movable]), spare
        for i in movable:
            addition = min(most - counts[i], max(1, left * portions[i] // whole), spare)
            counts[i] = counts[i] + addition
            spare = spare - addition
    return np.array(counts)


def centred(own_key, extent, deviation, most, cuts=(), kind=jnp.bfloat16):
    entries = deviation * jax.random.normal(own_key, extent, jnp.float32)
    if cuts:
        entries = entries * level_of(own_key, extent, cuts, -0.22, 0.18)
    return jnp.clip(entries, -most, most).astype(kind)


def setup_inputs(seed: int = 0) -> dict:
    splits = jax.random.split(jax.random.key(seed), 7)
    object_field = centred(splits[0], (2, NR, NC), 0.7, 5.0, ((1, 8), (2, 4)), jnp.float32)
    probe_field = centred(splits[1], (2, PATCH, PATCH), 0.7, 5.0, (), jnp.float32)
    owners_keys = jax.random.split(jax.random.fold_in(splits[2], 1), STEPS * POSITIONS // BATCH)
    owners_turns = jax.random.permutation(jax.random.fold_in(splits[2], 3), STEPS * POSITIONS // BATCH)
    owners = jax.vmap(lambda own, number: routed_block(jax.random.fold_in(splits[2], 2), own, number, BATCH, BANDS, 1, CAP, 2))(owners_keys, owners_turns).reshape((STEPS, POSITIONS, 1))
    row_offsets = place_ends(jax.random.randint(splits[3], (STEPS, POSITIONS), 0, TR), jax.random.fold_in(splits[3], 1), 0, TR - 1).astype(jnp.int32)
    col_offsets = place_ends(jax.random.randint(splits[4], (STEPS, POSITIONS), 0, TC), jax.random.fold_in(splits[4], 1), 0, TC - 1).astype(jnp.int32)
    intensities = jnp.clip(jnp.exp(math.log(3.0) - 3.4011974 * jax.random.uniform(splits[5], (STEPS, POSITIONS, PATCH, PATCH), jnp.float32) ** level_of(splits[5], (STEPS, POSITIONS, PATCH, PATCH), ((1, 32),), -0.2, 0.2)), 0.1, 3.0)
    return dict(object_field=object_field, probe_field=probe_field, owners=owners, row_offsets=row_offsets, col_offsets=col_offsets, intensities=intensities)


OBJECT_RATE = 0.25
PROBE_RATE = 1.0


def pattern_terms(patches, probe_wave, measured):
    exit_wave = probe_wave[None] * patches
    far_field = jnp.fft.fft2(exit_wave, norm="ortho")
    misfit = far_field.real * far_field.real + far_field.imag * far_field.imag - measured
    back_wave = jnp.fft.ifft2(misfit * far_field, norm="ortho")
    object_terms = jnp.conj(probe_wave)[None] * back_wave
    probe_term = jnp.sum(jnp.conj(patches) * back_wave, axis=0)
    return object_terms, probe_term


def reference(object_field, probe_field, owners, row_offsets, col_offsets, intensities):
    object_wave = object_field[0] + 1j * object_field[1]
    probe_wave = probe_field[0] + 1j * probe_field[1]
    counter = jnp.arange(POSITIONS, dtype=jnp.int32)
    strip_of = ((counter // BATCH) % STRIPS).astype(jnp.int32)
    for step_number in range(STEPS):
        owner_rows = owners[step_number, :, 0]
        top_rows = jnp.minimum(owner_rows * TR + row_offsets[step_number], NR - PATCH).astype(jnp.int32)
        left_cols = jnp.minimum(strip_of * TC + col_offsets[step_number], NC - PATCH).astype(jnp.int32)
        current_wave = object_wave
        current_probe = probe_wave

        def block_step(carry, block):
            object_grad, probe_grad = carry
            tops, lefts, measured = block

            def cut_one(top_row, left_col):
                return lax.dynamic_slice(current_wave, (top_row, left_col), (PATCH, PATCH))

            patches = jax.vmap(cut_one)(tops, lefts)
            object_terms, probe_term = pattern_terms(patches, current_probe, measured)

            def add_one(slot_number, total):
                corner = (tops[slot_number], lefts[slot_number])
                present_block = lax.dynamic_slice(total, corner, (PATCH, PATCH))
                return lax.dynamic_update_slice(total, present_block + object_terms[slot_number], corner)

            object_grad = lax.fori_loop(0, BATCH, add_one, object_grad)
            return (object_grad, probe_grad + probe_term), None

        blocks = (top_rows.reshape(-1, BATCH), left_cols.reshape(-1, BATCH),
                  intensities[step_number].reshape(-1, BATCH, PATCH, PATCH))
        start = (jnp.zeros_like(object_wave), jnp.zeros_like(probe_wave))
        (object_grad, probe_grad), unused = lax.scan(block_step, start, blocks)
        object_wave = object_wave - OBJECT_RATE * object_grad
        probe_wave = probe_wave - (PROBE_RATE / POSITIONS) * probe_grad
    return jnp.stack([object_wave.real, object_wave.imag]), jnp.stack([probe_wave.real, probe_wave.imag])
```

```python
import functools
import math

import jax
import jax.numpy as jnp
import ml_dtypes
import numpy as np
from jax import lax
from jax.experimental import pallas as pl
from jax.experimental.pallas import tpu as pltpu
from jax.sharding import PartitionSpec as P

CAP = 3
STEPS = 2
GROUP = 4
ROWS = 8

OBJECT_RATE = 0.25
PROBE_RATE = 1.0


def shifted(value, axis, steps):
    count = lax.axis_size(axis)
    leading, last = (max(0, -steps), min(count, count - steps))
    return lax.ppermute(value, axis, [(source, source + steps) for source in range(leading, last)])


def sum_everywhere(value, axes):
    for axis in axes:
        count = lax.axis_size(axis)
        step = 1
        while step < count:
            pairs = [(source, source ^ step) for source in range(count)]
            value = value + lax.ppermute(value, axis, pairs)
            step *= 2
    return value


def split_table(table):
    high = table.astype(ml_dtypes.bfloat16)
    low = (table - high.astype(np.float64)).astype(ml_dtypes.bfloat16)
    return high, low


def dft_tables(width):
    counter = np.arange(width)
    radians = (counter[:, None] * counter[None, :] % width) * (2.0 * math.pi / width)
    cos = np.cos(radians) / math.sqrt(width)
    sin = -np.sin(radians) / math.sqrt(width)
    plus = np.block([[cos, -sin], [sin, cos]])
    minus = np.block([[cos, sin], [-sin, cos]])

    def left(table):
        high, low = split_table(table)
        return np.concatenate([high, low, high], axis=1)

    def right(table):
        high, low = split_table(table)
        return np.concatenate([high, low, high], axis=0)

    return left(plus), right(minus), right(plus), left(minus)


def split(value):
    high = value.astype(jnp.bfloat16)
    low = (value - high.astype(jnp.float32)).astype(jnp.bfloat16)
    return high, low


def left_apply(table, parts):
    data = jnp.concatenate(
        [jnp.concatenate([re for re, _ in parts], axis=1), jnp.concatenate([im for _, im in parts], axis=1)],
        axis=0,
    )
    high, low = split(data)
    out = jnp.dot(table, jnp.concatenate([high, high, low], axis=0), preferred_element_type=jnp.float32)
    width = out.shape[0] // 2
    return [
        (out[:width, i * width : (i + 1) * width], out[width:, i * width : (i + 1) * width])
        for i in range(len(parts))
    ]


def right_apply(table, parts):
    data = jnp.concatenate([jnp.concatenate([re, im], axis=1) for re, im in parts], axis=0)
    high, low = split(data)
    out = jnp.dot(jnp.concatenate([high, high, low], axis=1), table, preferred_element_type=jnp.float32)
    width = out.shape[1] // 2
    return [
        (out[i * width : (i + 1) * width, :width], out[i * width : (i + 1) * width, width:])
        for i in range(len(parts))
    ]


def step_kernel(
    tops, lefts, extended, probe, measured, table_a, table_b, table_c, table_d, gradient, probe_gradient
):
    width = probe.shape[1]
    slots = measured.shape[0]
    gradient[...] = jnp.zeros_like(gradient)
    probe_gradient[...] = jnp.zeros_like(probe_gradient)
    tiles = width // ROWS
    lane = lax.broadcasted_iota(jnp.int32, (tiles + 1, ROWS, width), 2)
    row = lax.broadcasted_iota(jnp.int32, (tiles, ROWS, width), 1)

    def corner(slot):
        top = jnp.maximum(tops[slot], 0)
        left = lefts[slot]
        top_base = pl.multiple_of(top // ROWS * ROWS, ROWS)
        left_base = pl.multiple_of(left // width * width, width)
        return top_base, top - top_base, left_base, left - left_base

    def cut(slot):
        top_base, down, left_base, off = corner(slot)
        rows = pl.ds(top_base, width + ROWS)
        out = []
        for part in range(2):
            near = extended[part, rows, pl.ds(left_base, width)].reshape(lane.shape)
            far = extended[part, rows, pl.ds(left_base + width, width)].reshape(lane.shape)
            value = pltpu.roll(jnp.where(lane < off, far, near), lax.rem(width - off, width), 2)
            value = pltpu.roll(value, lax.rem(ROWS - down, ROWS), 1)
            value = jnp.where(row < ROWS - down, value[:tiles], value[1:])
            out.append(value.reshape(width, width))
        return out

    def add(slot, terms):
        top_base, down, left_base, off = corner(slot)
        rows = pl.ds(top_base, width + ROWS)
        for part in range(2):
            value = pltpu.roll(terms[part].reshape(row.shape), down, 1)
            value = pltpu.roll(value, off, 2)
            upper = jnp.where(row >= down, value, 0.0)
            lower = jnp.where(row >= down, 0.0, value)
            edge = jnp.zeros((1, ROWS, width), jnp.float32)
            value = jnp.concatenate([upper, edge], axis=0) + jnp.concatenate([edge, lower], axis=0)
            near = jnp.where(lane < off, 0.0, value).reshape(width + ROWS, width)
            far = jnp.where(lane < off, value, 0.0).reshape(width + ROWS, width)
            gradient[part, rows, pl.ds(left_base, width)] += near
            gradient[part, rows, pl.ds(left_base + width, width)] += far

    def body(group, carry):
        pairs = [
            [group * GROUP + 2 * pair, group * GROUP + 2 * pair + 1] for pair in range(GROUP // 2)
        ]
        for pair in pairs:
            patches = [cut(slot) for slot in pair]
            probe_re, probe_im = probe[0], probe[1]
            waves = [
                (probe_re * re - probe_im * im, probe_re * im + probe_im * re) for re, im in patches
            ]
            far = right_apply(table_b[...], left_apply(table_a[...], waves))
            scaled = []
            for slot, (re, im) in zip(pair, far):
                filled = jnp.where(tops[slot] >= 0, 1.0, 0.0)
                misfit = (re * re + im * im - measured[slot]) * filled
                scaled.append((misfit * re, misfit * im))
            back = left_apply(table_d[...], right_apply(table_c[...], scaled))
            probe_terms = [
                (qr * br + qi * bi, qr * bi - qi * br) for (qr, qi), (br, bi) in zip(patches, back)
            ]
            probe_gradient[0] += probe_terms[0][0] + probe_terms[1][0]
            probe_gradient[1] += probe_terms[0][1] + probe_terms[1][1]
            for slot, (br, bi) in zip(pair, back):
                add(slot, (probe_re * br + probe_im * bi, probe_re * bi - probe_im * br))
        return carry

    lax.fori_loop(0, slots // GROUP, body, 0)


def run_step(tops, lefts, extended, probe, measured, tables):
    vmem = pl.BlockSpec(memory_space=pltpu.VMEM)
    smem = pl.BlockSpec(memory_space=pltpu.SMEM)
    width = probe.shape[1]
    slots = measured.shape[0]
    return pl.pallas_call(
        step_kernel,
        out_shape=(
            jax.ShapeDtypeStruct(extended.shape, jnp.float32),
            jax.ShapeDtypeStruct(probe.shape, jnp.float32),
        ),
        in_specs=[smem, smem] + [vmem] * 7,
        out_specs=(vmem, vmem),
        compiler_params=pltpu.CompilerParams(vmem_limit_bytes=40 * 1024 * 1024),
        cost_estimate=pl.CostEstimate(
            flops=slots * 24 * 8 * width**3, bytes_accessed=8 * 1024 * 1024, transcendentals=0
        ),
    )(tops, lefts, extended, probe, measured, *tables)


def extend_tile(object_field, width):
    right_part = shifted(object_field[:, :, :width], "tx", -1)
    widened = jnp.concatenate([object_field, right_part], axis=2)
    lower_part = shifted(widened[:, :width, :], "ty", -1)
    return jnp.concatenate([widened, lower_part], axis=1)


def sum_extended(total, tile_rows, tile_cols, width):
    from_left = shifted(total[:, :, tile_cols:], "tx", 1)
    from_right = shifted(total[:, :, :width], "tx", -1)
    total = jnp.concatenate(
        [
            total[:, :, :width] + from_left,
            total[:, :, width:tile_cols],
            total[:, :, tile_cols:] + from_right,
        ],
        axis=2,
    )
    from_above = shifted(total[:, tile_rows:, :], "ty", 1)
    from_below = shifted(total[:, :width, :], "ty", -1)
    return jnp.concatenate(
        [
            total[:, :width, :] + from_above,
            total[:, width:tile_rows, :],
            total[:, tile_rows:, :] + from_below,
        ],
        axis=1,
    )


def fold_back(total, tile_rows, tile_cols, width):
    spill_down = shifted(total[:, tile_rows:, :], "ty", 1)
    upper_part = total[:, :tile_rows, :]
    upper_part = jnp.concatenate(
        [upper_part[:, :width, :] + spill_down, upper_part[:, width:, :]], axis=1
    )
    spill_right = shifted(upper_part[:, :, tile_cols:], "tx", 1)
    return jnp.concatenate(
        [upper_part[:, :, :width] + spill_right, upper_part[:, :, width:tile_cols]], axis=2
    )


def on_device(object_field, probe_field, owners, row_offsets, col_offsets, intensities):
    band_count = lax.axis_size("ty")
    strip_count = lax.axis_size("tx")
    tile_rows = object_field.shape[1]
    tile_cols = object_field.shape[2]
    width = probe_field.shape[1]
    batch_rows = row_offsets.shape[1]
    slot_count = band_count * CAP
    strip_index = lax.axis_index("tx")
    tables = [jnp.asarray(table) for table in dft_tables(width)]
    probe_scale = PROBE_RATE / (batch_rows * band_count * strip_count)

    owner_rows = owners[:, :, 0]
    position_ids = jnp.arange(batch_rows, dtype=jnp.int32)
    earlier = (owner_rows[:, None, :] == owner_rows[:, :, None]) & (
        position_ids[None, None, :] < position_ids[None, :, None]
    )
    slot_of = owner_rows * CAP + jnp.sum(earlier.astype(jnp.int32), axis=2)
    top_local = (
        jnp.minimum(owner_rows * tile_rows + row_offsets, tile_rows * band_count - width)
        - owner_rows * tile_rows
    )
    left_local = (
        jnp.minimum(strip_index * tile_cols + col_offsets, tile_cols * strip_count - width)
        - strip_index * tile_cols
    )
    slot_ids = jnp.arange(slot_count, dtype=jnp.int32)
    matches = slot_of[:, None, :] == slot_ids[None, :, None]
    filled = jnp.any(matches, axis=2)

    def by_slot(values):
        return jnp.sum(jnp.where(matches, values[:, None, :], 0), axis=2)

    want_top = jnp.where(filled, by_slot(top_local), -1)
    want_left = by_slot(left_local)
    holder = by_slot(jnp.broadcast_to(position_ids[None], slot_of.shape))
    wanted = jnp.stack([want_top, want_left]).reshape(2 * STEPS, band_count, CAP)
    received = lax.all_to_all(wanted, "ty", split_axis=1, concat_axis=1, tiled=True).reshape(
        2, STEPS, slot_count
    )

    def exchange(step_number):
        chosen = jnp.take(intensities[step_number], holder[step_number], axis=0, mode="clip")
        moved = lax.all_to_all(
            chosen.reshape(band_count, CAP, width, width), "ty", split_axis=0, concat_axis=0, tiled=True
        )
        return moved.reshape(slot_count, width, width)

    measured = [exchange(step_number) for step_number in range(STEPS)]
    extended = extend_tile(object_field, width)
    for step_number in range(STEPS):
        gathered, probe_term = run_step(
            received[0, step_number],
            received[1, step_number],
            extended,
            probe_field,
            measured[step_number],
            tables,
        )
        probe_total = sum_everywhere(probe_term, ("ty", "tx"))
        if step_number < STEPS - 1:
            extended = extended - OBJECT_RATE * sum_extended(gathered, tile_rows, tile_cols, width)
        else:
            object_field = extended[:, :tile_rows, :tile_cols] - OBJECT_RATE * fold_back(
                gathered, tile_rows, tile_cols, width
            )
        probe_field = probe_field - probe_scale * probe_total
    return (object_field, probe_field)


def solution(mesh):
    in_specs = (
        P(None, "ty", "tx"),
        P(),
        P(None, ("ty", "tx"), None),
        P(None, ("ty", "tx")),
        P(None, ("ty", "tx")),
        P(None, ("ty", "tx"), None, None),
    )
    out_specs = (P(None, "ty", "tx"), P())
    return jax.shard_map(
        on_device, mesh=mesh, in_specs=in_specs, out_specs=out_specs, check_vma=False
    )
```

```python
import functools
import math

import jax
import jax.numpy as jnp
import ml_dtypes
import numpy as np
from jax import lax
from jax.experimental import pallas as pl
from jax.experimental.pallas import tpu as pltpu
from jax.sharding import PartitionSpec as P

CAP = 3
STEPS = 2
GROUP = 4
ROWS = 8

OBJECT_RATE = 0.25
PROBE_RATE = 1.0


def split_table(table):
    high = table.astype(ml_dtypes.bfloat16)
    low = (table - high.astype(np.float64)).astype(ml_dtypes.bfloat16)
    return high, low


def dft_tables(width):
    counter = np.arange(width)
    radians = (counter[:, None] * counter[None, :] % width) * (2.0 * math.pi / width)
    cos = np.cos(radians) / math.sqrt(width)
    sin = -np.sin(radians) / math.sqrt(width)
    plus = np.block([[cos, -sin], [sin, cos]])
    minus = np.block([[cos, sin], [-sin, cos]])

    def left(table):
        high, low = split_table(table)
        return np.concatenate([high, low, high], axis=1)

    def right(table):
        high, low = split_table(table)
        return np.concatenate([high, low, high], axis=0)

    return np.stack([left(plus), left(minus)]), np.stack([right(minus), right(plus)])


def split(value):
    high = value.astype(jnp.bfloat16)
    low = (value - high.astype(jnp.float32)).astype(jnp.bfloat16)
    return high, low


def left_apply(table, parts):
    data = jnp.concatenate(
        [jnp.concatenate([re for re, _ in parts], axis=1), jnp.concatenate([im for _, im in parts], axis=1)],
        axis=0,
    )
    high, low = split(data)
    out = jnp.dot(table, jnp.concatenate([high, high, low], axis=0), preferred_element_type=jnp.float32)
    width = out.shape[0] // 2
    return [
        (out[:width, i * width : (i + 1) * width], out[width:, i * width : (i + 1) * width])
        for i in range(len(parts))
    ]


def right_apply(table, parts):
    data = jnp.concatenate([jnp.concatenate([re, im], axis=1) for re, im in parts], axis=0)
    high, low = split(data)
    out = jnp.dot(jnp.concatenate([high, high, low], axis=1), table, preferred_element_type=jnp.float32)
    width = out.shape[1] // 2
    return [
        (out[i * width : (i + 1) * width, :width], out[i * width : (i + 1) * width, width:])
        for i in range(len(parts))
    ]


def step_kernel(
    tops, lefts, extended, probe, measured, left_tables, right_tables, gradient, probe_gradient
):
    width = probe.shape[1]
    slots = measured.shape[0]
    gradient[...] = jnp.zeros_like(gradient)
    probe_gradient[...] = jnp.zeros_like(probe_gradient)
    tiles = width // ROWS
    lane = lax.broadcasted_iota(jnp.int32, (tiles + 1, ROWS, width), 2)
    row = lax.broadcasted_iota(jnp.int32, (tiles, ROWS, width), 1)

    def corner(slot):
        top = jnp.maximum(tops[slot], 0)
        left = lefts[slot]
        top_base = pl.multiple_of(top // ROWS * ROWS, ROWS)
        left_base = pl.multiple_of(left // width * width, width)
        return top_base, top - top_base, left_base, left - left_base

    def cut(slot):
        top_base, down, left_base, off = corner(slot)
        rows = pl.ds(top_base, width + ROWS)
        out = []
        for part in range(2):
            near = extended[part, rows, pl.ds(left_base, width)].reshape(lane.shape)
            far = extended[part, rows, pl.ds(left_base + width, width)].reshape(lane.shape)
            value = pltpu.roll(jnp.where(lane < off, far, near), lax.rem(width - off, width), 2)
            value = pltpu.roll(value, lax.rem(ROWS - down, ROWS), 1)
            value = jnp.where(row < ROWS - down, value[:tiles], value[1:])
            out.append(value.reshape(width, width))
        return out

    def add(slot, terms):
        top_base, down, left_base, off = corner(slot)
        rows = pl.ds(top_base, width + ROWS)
        for part in range(2):
            value = pltpu.roll(terms[part].reshape(row.shape), down, 1)
            value = pltpu.roll(value, off, 2)
            upper = jnp.where(row >= down, value, 0.0)
            lower = jnp.where(row >= down, 0.0, value)
            edge = jnp.zeros((1, ROWS, width), jnp.float32)
            value = jnp.concatenate([upper, edge], axis=0) + jnp.concatenate([edge, lower], axis=0)
            near = jnp.where(lane < off, 0.0, value).reshape(width + ROWS, width)
            far = jnp.where(lane < off, value, 0.0).reshape(width + ROWS, width)
            gradient[part, rows, pl.ds(left_base, width)] += near
            gradient[part, rows, pl.ds(left_base + width, width)] += far

    def body(group, carry):
        pairs = [
            [group * GROUP + 2 * pair, group * GROUP + 2 * pair + 1] for pair in range(GROUP // 2)
        ]
        for pair in pairs:
            patches = [cut(slot) for slot in pair]
            probe_re, probe_im = probe[0], probe[1]
            waves = [
                (probe_re * re - probe_im * im, probe_re * im + probe_im * re) for re, im in patches
            ]
            far = right_apply(right_tables[0], left_apply(left_tables[0], waves))
            scaled = []
            for slot, (re, im) in zip(pair, far):
                filled = jnp.where(tops[slot] >= 0, 1.0, 0.0)
                misfit = (re * re + im * im - measured[slot]) * filled
                scaled.append((misfit * re, misfit * im))
            back = left_apply(left_tables[1], right_apply(right_tables[1], scaled))
            probe_terms = [
                (qr * br + qi * bi, qr * bi - qi * br) for (qr, qi), (br, bi) in zip(patches, back)
            ]
            probe_gradient[0] += probe_terms[0][0] + probe_terms[1][0]
            probe_gradient[1] += probe_terms[0][1] + probe_terms[1][1]
            for slot, (br, bi) in zip(pair, back):
                add(slot, (probe_re * br + probe_im * bi, probe_re * bi - probe_im * br))
        return carry

    lax.fori_loop(0, slots // GROUP, body, 0)


def run_step(tops, lefts, extended, probe, measured, tables):
    vmem = pl.BlockSpec(memory_space=pltpu.VMEM)
    smem = pl.BlockSpec(memory_space=pltpu.SMEM)
    width = probe.shape[1]
    slots = measured.shape[0]
    return pl.pallas_call(
        step_kernel,
        out_shape=(
            jax.ShapeDtypeStruct(extended.shape, jnp.float32),
            jax.ShapeDtypeStruct(probe.shape, jnp.float32),
        ),
        in_specs=[smem, smem] + [vmem] * 5,
        out_specs=(vmem, vmem),
        compiler_params=pltpu.CompilerParams(vmem_limit_bytes=40 * 1024 * 1024),
        cost_estimate=pl.CostEstimate(
            flops=slots * 24 * 8 * width**3, bytes_accessed=8 * 1024 * 1024, transcendentals=0
        ),
    )(tops, lefts, extended, probe, measured, *tables)


def remote(source, target, send, receive, ty, tx):
    return pltpu.make_async_remote_copy(
        src_ref=source,
        dst_ref=target,
        send_sem=send,
        recv_sem=receive,
        device_id=(ty, tx),
        device_id_type=pl.DeviceIdType.MESH,
    )


def only(condition):
    return pl.when(condition)


def greet(partners):
    barrier = pltpu.get_barrier_semaphore()
    count = 0
    for exists, ty, tx in partners:

        def signal(ty=ty, tx=tx):
            pl.semaphore_signal(
                barrier, inc=1, device_id=(ty, tx), device_id_type=pl.DeviceIdType.MESH
            )

        if exists is True:
            signal()
            count = count + 1
        else:
            only(exists)(signal)
            count = count + exists.astype(jnp.int32)
    pl.semaphore_wait(barrier, count)


def peers(band_count, ty, tx):
    return [(True, lax.rem(ty + k, band_count), tx) for k in range(1, band_count)]


def stage_measured(step_number, intensities, holder, staged, outgoing, measured, load_sem, ty):
    load = pltpu.make_async_copy(intensities.at[step_number], staged, load_sem)
    load.start()
    load.wait()

    def place(slot, carry):
        outgoing[slot] = staged[holder[step_number, slot]]
        return carry

    lax.fori_loop(0, outgoing.shape[0], place, 0)
    for own in range(CAP):
        measured[ty * CAP + own] = staged[holder[step_number, ty * CAP + own]]


def measured_copies(band_count, outgoing, measured, send_sems, recv_sems, ty, tx):
    copies = []
    for k in range(1, band_count):
        peer = lax.rem(ty + k, band_count)
        copies.append(
            remote(
                outgoing.at[pl.ds(peer * CAP, CAP)],
                measured.at[pl.ds(ty * CAP, CAP)],
                send_sems.at[k - 1],
                recv_sems.at[k - 1],
                peer,
                tx,
            )
        )
    return copies


def begin_kernel(
    sizes, holder, intensities, object_field, wants, measured, extended, received,
    staged, outgoing, load_sem, own_sem, send_sems, recv_sems, want_send, want_recv, halo_send, halo_recv,
):
    band_count, strip_count, width = sizes
    ty, tx = lax.axis_index("ty"), lax.axis_index("tx")
    rows, cols = object_field.shape[1:]
    above, left = ty > 0, tx > 0
    below, right = ty < band_count - 1, tx < strip_count - 1
    own = pltpu.make_async_copy(object_field, extended.at[:, :rows, :cols], own_sem)
    own.start()
    greet(
        peers(band_count, ty, tx)
        + [
            (left, ty, tx - 1),
            (right, ty, tx + 1),
            (above & left, ty - 1, tx - 1),
            (below & right, ty + 1, tx + 1),
        ]
    )
    want_copies = []
    for k in range(1, band_count):
        peer = lax.rem(ty + k, band_count)
        want_copies.append(
            remote(wants.at[peer], received.at[ty], want_send.at[k - 1], want_recv.at[k - 1], peer, tx)
        )
    for copy in want_copies:
        copy.start()
    halos = [
        (
            left, right,
            remote(object_field.at[:, :, :width], extended.at[:, :rows, cols:],
                   halo_send.at[0], halo_recv.at[0], ty, tx - 1),
        ),
        (
            above, below,
            remote(object_field.at[:, :width, :], extended.at[:, rows:, :cols],
                   halo_send.at[1], halo_recv.at[1], ty - 1, tx),
        ),
        (
            above & left, below & right,
            remote(object_field.at[:, :width, :width], extended.at[:, rows:, cols:],
                   halo_send.at[2], halo_recv.at[2], ty - 1, tx - 1),
        ),
    ]
    for sends, _, copy in halos:
        only(sends)(copy.start)
    stage_measured(0, intensities, holder, staged, outgoing, measured, load_sem, ty)
    copies = measured_copies(band_count, outgoing, measured, send_sems, recv_sems, ty, tx)
    for copy in copies:
        copy.start()
    received[ty] = wants[ty]

    @only(jnp.logical_not(right))
    def _():
        extended[:, :rows, cols:] = jnp.zeros((2, rows, width), jnp.float32)

    @only(jnp.logical_not(below))
    def _():
        extended[:, rows:, :cols] = jnp.zeros((2, width, cols), jnp.float32)

    @only(jnp.logical_not(below & right))
    def _():
        extended[:, rows:, cols:] = jnp.zeros((2, width, width), jnp.float32)

    own.wait()
    for copy in want_copies:
        copy.wait()
    for sends, receives, copy in halos:
        only(sends)(copy.wait_send)
        only(receives)(copy.wait_recv)
    for copy in copies:
        copy.wait()


def butterfly(band_count, strip_count, ty, tx):
    partners = []
    step = 1
    while step < strip_count:
        partners.append(("tx", step, (ty, tx + step * (1 - 2 * (tx // step % 2)))))
        step *= 2
    step = 1
    while step < band_count:
        partners.append(("ty", step, (ty + step * (1 - 2 * (ty // step % 2)), tx)))
        step *= 2
    return partners


def probe_rounds(partners, probe_term, sums, arrived, send_sems, recv_sems):
    def source(k):
        return probe_term if k == 0 else sums.at[k - 1]

    copies = [
        remote(source(k), arrived.at[k], send_sems.at[k], recv_sems.at[k], *partner)
        for k, (_, _, partner) in enumerate(partners)
    ]

    def finish(k):
        copies[k].wait()
        sums[k] = source(k)[...] + arrived[k]

    return copies, finish


def middle_kernel(
    sizes, scale, holder, intensities, gradient, probe_term, extended, probe, measured, new_extended, new_probe,
    staged, outgoing, load_sem, send_sems, recv_sems, side, ends, ends_out, side_send, side_recv, end_send, end_recv,
    sums, arrived, sum_send, sum_recv,
):
    band_count, strip_count, width = sizes
    ty, tx = lax.axis_index("ty"), lax.axis_index("tx")
    rows, cols = (size - width for size in extended.shape[1:])
    above, left = ty > 0, tx > 0
    below, right = ty < band_count - 1, tx < strip_count - 1
    partners = butterfly(band_count, strip_count, ty, tx)
    greet(
        peers(band_count, ty, tx)
        + [(left, ty, tx - 1), (right, ty, tx + 1)]
        + [(True, *partner) for axis, step, partner in partners if axis == "tx" and step > 1]
    )
    copies, finish = probe_rounds(partners, probe_term, sums, arrived, sum_send, sum_recv)
    copies[0].start()
    sides = [
        (right, left, remote(gradient.at[:, :, cols:], side.at[0], side_send.at[0], side_recv.at[0], ty, tx + 1)),
        (left, right, remote(gradient.at[:, :, :width], side.at[1], side_send.at[1], side_recv.at[1], ty, tx - 1)),
    ]
    for sends, _, copy in sides:
        only(sends)(copy.start)
    stage_measured(1, intensities, holder, staged, outgoing, measured, load_sem, ty)
    measured_sends = measured_copies(band_count, outgoing, measured, send_sems, recv_sems, ty, tx)
    for copy in measured_sends:
        copy.start()
    for number, (_, receives, _) in enumerate(sides):

        @only(jnp.logical_not(receives))
        def _(number=number):
            side[number] = jnp.zeros(side.shape[1:], jnp.float32)

    for k in range(len(copies)):
        finish(k)
        if k + 1 < len(copies):
            copies[k + 1].start()
    new_probe[...] = probe[...] - scale * sums[len(copies) - 1]
    for sends, receives, copy in sides:
        only(sends)(copy.wait_send)
        only(receives)(copy.wait_recv)
    for number, first in enumerate((rows, 0)):
        block = pl.ds(first, width)
        ends_out[number, :, :, :width] = gradient[:, block, :width] + side[0, :, block, :]
        ends_out[number, :, :, width:cols] = gradient[:, block, width:cols]
        ends_out[number, :, :, cols:] = gradient[:, block, cols:] + side[1, :, block, :]
    end_copies = [
        (below, above, remote(ends_out.at[0], ends.at[0], end_send.at[0], end_recv.at[0], ty + 1, tx)),
        (above, below, remote(ends_out.at[1], ends.at[1], end_send.at[1], end_recv.at[1], ty - 1, tx)),
    ]
    for sends, _, copy in end_copies:
        only(sends)(copy.start)
    for number, (_, receives, _) in enumerate(end_copies):

        @only(jnp.logical_not(receives))
        def _(number=number):
            ends[number] = jnp.zeros(ends.shape[1:], jnp.float32)

    inner = pl.ds(width, rows - width)
    new_extended[:, inner, :width] = extended[:, inner, :width] - OBJECT_RATE * (
        gradient[:, inner, :width] + side[0, :, inner, :]
    )
    new_extended[:, inner, width:cols] = (
        extended[:, inner, width:cols] - OBJECT_RATE * gradient[:, inner, width:cols]
    )
    new_extended[:, inner, cols:] = extended[:, inner, cols:] - OBJECT_RATE * (
        gradient[:, inner, cols:] + side[1, :, inner, :]
    )
    for sends, receives, copy in end_copies:
        only(sends)(copy.wait_send)
        only(receives)(copy.wait_recv)
    new_extended[:, :width, :] = extended[:, :width, :] - OBJECT_RATE * (ends_out[1] + ends[0])
    new_extended[:, rows:, :] = extended[:, rows:, :] - OBJECT_RATE * (ends_out[0] + ends[1])
    for copy in measured_sends:
        copy.wait()


def end_kernel(
    sizes, scale, gradient, probe_term, extended, probe, new_object, new_probe,
    side, end, corner, halo_send, halo_recv, sums, arrived, sum_send, sum_recv,
):
    band_count, strip_count, width = sizes
    ty, tx = lax.axis_index("ty"), lax.axis_index("tx")
    rows, cols = new_object.shape[1:]
    above, left = ty > 0, tx > 0
    below, right = ty < band_count - 1, tx < strip_count - 1
    partners = butterfly(band_count, strip_count, ty, tx)
    greet(
        [
            (left, ty, tx - 1),
            (right, ty, tx + 1),
            (above, ty - 1, tx),
            (below, ty + 1, tx),
            (above & left, ty - 1, tx - 1),
            (below & right, ty + 1, tx + 1),
        ]
        + [(True, *partner) for _, step, partner in partners if step > 1]
    )
    copies, finish = probe_rounds(partners, probe_term, sums, arrived, sum_send, sum_recv)
    copies[0].start()
    halos = [
        (right, left, side, remote(gradient.at[:, :rows, cols:], side, halo_send.at[0], halo_recv.at[0], ty, tx + 1)),
        (below, above, end, remote(gradient.at[:, rows:, :cols], end, halo_send.at[1], halo_recv.at[1], ty + 1, tx)),
        (
            below & right, above & left, corner,
            remote(gradient.at[:, rows:, cols:], corner, halo_send.at[2], halo_recv.at[2], ty + 1, tx + 1),
        ),
    ]
    for sends, _, _, copy in halos:
        only(sends)(copy.start)
    for _, receives, target, _ in halos:

        @only(jnp.logical_not(receives))
        def _(target=target):
            target[...] = jnp.zeros(target.shape, jnp.float32)

    new_object[:, width:, width:] = (
        extended[:, width:rows, width:cols] - OBJECT_RATE * gradient[:, width:rows, width:cols]
    )
    for k in range(len(copies)):
        finish(k)
        if k + 1 < len(copies):
            copies[k + 1].start()
    new_probe[...] = probe[...] - scale * sums[len(copies) - 1]
    for sends, receives, _, copy in halos:
        only(sends)(copy.wait_send)
        only(receives)(copy.wait_recv)
    new_object[:, width:, :width] = extended[:, width:rows, :width] - OBJECT_RATE * (
        gradient[:, width:rows, :width] + side[:, width:, :]
    )
    new_object[:, :width, width:] = extended[:, :width, width:cols] - OBJECT_RATE * (
        gradient[:, :width, width:cols] + end[:, :, width:]
    )
    new_object[:, :width, :width] = extended[:, :width, :width] - OBJECT_RATE * (
        gradient[:, :width, :width] + side[:, :width, :] + end[:, :, :width] + corner[...]
    )


VMEM = pl.BlockSpec(memory_space=pltpu.VMEM)
SMEM = pl.BlockSpec(memory_space=pltpu.SMEM)
HBM = pl.BlockSpec(memory_space=pl.ANY)
DMA = pltpu.SemaphoreType.DMA


def floats(*shape):
    return jax.ShapeDtypeStruct(shape, jnp.float32)


def communicate(kernel, number, in_specs, shapes, scratch):
    return pl.pallas_call(
        kernel,
        out_shape=shapes,
        in_specs=in_specs,
        out_specs=tuple(VMEM for _ in shapes),
        scratch_shapes=scratch,
        compiler_params=pltpu.CompilerParams(
            collective_id=number, has_side_effects=True, vmem_limit_bytes=48 * 1024 * 1024
        ),
    )


def on_device(object_field, probe_field, owners, row_offsets, col_offsets, intensities):
    band_count = lax.axis_size("ty")
    strip_count = lax.axis_size("tx")
    tile_rows = object_field.shape[1]
    tile_cols = object_field.shape[2]
    width = probe_field.shape[1]
    batch_rows = row_offsets.shape[1]
    slot_count = band_count * CAP
    strip_index = lax.axis_index("tx")
    tables = [jnp.asarray(table) for table in dft_tables(width)]
    probe_scale = PROBE_RATE / (batch_rows * band_count * strip_count)

    owner_rows = owners[:, :, 0]
    position_ids = jnp.arange(batch_rows, dtype=jnp.int32)
    earlier = (owner_rows[:, None, :] == owner_rows[:, :, None]) & (
        position_ids[None, None, :] < position_ids[None, :, None]
    )
    slot_of = owner_rows * CAP + jnp.sum(earlier.astype(jnp.int32), axis=2)
    top_local = (
        jnp.minimum(owner_rows * tile_rows + row_offsets, tile_rows * band_count - width)
        - owner_rows * tile_rows
    )
    left_local = (
        jnp.minimum(strip_index * tile_cols + col_offsets, tile_cols * strip_count - width)
        - strip_index * tile_cols
    )
    slot_ids = jnp.arange(slot_count, dtype=jnp.int32)
    matches = slot_of[:, None, :] == slot_ids[None, :, None]
    filled = jnp.any(matches, axis=2)

    def by_slot(values):
        return jnp.sum(jnp.where(matches, values[:, None, :], 0), axis=2)

    want_top = jnp.where(filled, by_slot(top_local), -1)
    want_left = by_slot(left_local)
    holder = by_slot(jnp.broadcast_to(position_ids[None], slot_of.shape))
    sizes = (band_count, strip_count, width)
    wants = jnp.concatenate([want_top, want_left]).reshape(2 * STEPS, band_count, CAP).transpose(1, 0, 2)
    wants = jnp.pad(wants, ((0, 0), (0, 8 - 2 * STEPS), (0, 128 - CAP)))
    staging = [
        pltpu.VMEM((batch_rows, width, width), jnp.float32),
        pltpu.VMEM((slot_count, width, width), jnp.float32),
        DMA,
    ]
    pair_sems = [DMA((band_count - 1,)), DMA((band_count - 1,))]
    measured, extended, received = communicate(
        functools.partial(begin_kernel, sizes),
        0,
        [SMEM, HBM, HBM, VMEM],
        (
            floats(slot_count, width, width),
            floats(2, tile_rows + width, tile_cols + width),
            jax.ShapeDtypeStruct(wants.shape, jnp.int32),
        ),
        staging + [DMA] + pair_sems + pair_sems + [DMA((3,)), DMA((3,))],
    )(holder, intensities, object_field, wants)
    received = received[:, : 2 * STEPS, :CAP].transpose(1, 0, 2).reshape(2, STEPS, slot_count)
    rounds = (band_count * strip_count).bit_length() - 1
    summing = [
        pltpu.VMEM((rounds, 2, width, width), jnp.float32),
        pltpu.VMEM((rounds, 2, width, width), jnp.float32),
        DMA((rounds,)),
        DMA((rounds,)),
    ]
    gradient, probe_term = run_step(received[0, 0], received[1, 0], extended, probe_field, measured, tables)
    measured, extended, probe_field = communicate(
        functools.partial(middle_kernel, sizes, probe_scale),
        1,
        [SMEM, HBM] + [VMEM] * 4,
        (floats(*measured.shape), floats(*extended.shape), floats(*probe_field.shape)),
        staging
        + pair_sems
        + [
            pltpu.VMEM((2, 2, tile_rows + width, width), jnp.float32),
            pltpu.VMEM((2, 2, width, tile_cols + width), jnp.float32),
            pltpu.VMEM((2, 2, width, tile_cols + width), jnp.float32),
        ]
        + [DMA((2,))] * 4
        + summing,
    )(holder, intensities, gradient, probe_term, extended, probe_field)
    gradient, probe_term = run_step(received[0, 1], received[1, 1], extended, probe_field, measured, tables)
    return communicate(
        functools.partial(end_kernel, sizes, probe_scale),
        2,
        [VMEM] * 4,
        (floats(*object_field.shape), floats(*probe_field.shape)),
        [
            pltpu.VMEM((2, tile_rows, width), jnp.float32),
            pltpu.VMEM((2, width, tile_cols), jnp.float32),
            pltpu.VMEM((2, width, width), jnp.float32),
            DMA((3,)),
            DMA((3,)),
        ]
        + summing,
    )(gradient, probe_term, extended, probe_field)


def solution(mesh):
    in_specs = (
        P(None, "ty", "tx"),
        P(),
        P(None, ("ty", "tx"), None),
        P(None, ("ty", "tx")),
        P(None, ("ty", "tx")),
        P(None, ("ty", "tx"), None, None),
    )
    out_specs = (P(None, "ty", "tx"), P())
    return jax.shard_map(
        on_device, mesh=mesh, in_specs=in_specs, out_specs=out_specs, check_vma=False
    )
```

```python
import functools
import math

import jax
import jax.numpy as jnp
import ml_dtypes
import numpy as np
from jax import lax
from jax.experimental import pallas as pl
from jax.experimental.pallas import tpu as pltpu
from jax.sharding import PartitionSpec as P

CAP = 3
STEPS = 2
GROUP = 4
ROWS = 8

OBJECT_RATE = 0.25
PROBE_RATE = 1.0


def split_table(table):
    high = table.astype(ml_dtypes.bfloat16)
    low = (table - high.astype(np.float64)).astype(ml_dtypes.bfloat16)
    return high, low


def dft_tables(width):
    counter = np.arange(width)
    radians = (counter[:, None] * counter[None, :] % width) * (2.0 * math.pi / width)
    cos = np.cos(radians) / math.sqrt(width)
    sin = -np.sin(radians) / math.sqrt(width)
    plus = np.block([[cos, -sin], [sin, cos]])
    minus = np.block([[cos, sin], [-sin, cos]])

    def left(table):
        high, low = split_table(table)
        return np.concatenate([high, low, high], axis=1)

    def right(table):
        high, low = split_table(table)
        return np.concatenate([high, low, high], axis=0)

    return np.stack([left(plus), left(minus)]), np.stack([right(minus), right(plus)])


def split(value):
    high = value.astype(jnp.bfloat16)
    low = (value - high.astype(jnp.float32)).astype(jnp.bfloat16)
    return high, low


def left_apply(table, parts):
    data = jnp.concatenate(
        [jnp.concatenate([re for re, _ in parts], axis=1), jnp.concatenate([im for _, im in parts], axis=1)],
        axis=0,
    )
    high, low = split(data)
    out = jnp.dot(table, jnp.concatenate([high, high, low], axis=0), preferred_element_type=jnp.float32)
    width = out.shape[0] // 2
    return [
        (out[:width, i * width : (i + 1) * width], out[width:, i * width : (i + 1) * width])
        for i in range(len(parts))
    ]


def right_apply(table, parts):
    data = jnp.concatenate([jnp.concatenate([re, im], axis=1) for re, im in parts], axis=0)
    high, low = split(data)
    out = jnp.dot(jnp.concatenate([high, high, low], axis=1), table, preferred_element_type=jnp.float32)
    width = out.shape[1] // 2
    return [
        (out[i * width : (i + 1) * width, :width], out[i * width : (i + 1) * width, width:])
        for i in range(len(parts))
    ]


def step_kernel(
    tops, lefts, extended, probe, measured, left_tables, right_tables, gradient, probe_gradient
):
    width = probe.shape[1]
    slots = measured.shape[0]
    gradient[...] = jnp.zeros_like(gradient)
    probe_gradient[...] = jnp.zeros_like(probe_gradient)
    tiles = width // ROWS
    lane = lax.broadcasted_iota(jnp.int32, (tiles + 1, ROWS, width), 2)
    row = lax.broadcasted_iota(jnp.int32, (tiles, ROWS, width), 1)

    def corner(slot):
        top = jnp.maximum(tops[slot], 0)
        left = lefts[slot]
        top_base = pl.multiple_of(top // ROWS * ROWS, ROWS)
        left_base = pl.multiple_of(left // width * width, width)
        return top_base, top - top_base, left_base, left - left_base

    def cut(slot):
        top_base, down, left_base, off = corner(slot)
        rows = pl.ds(top_base, width + ROWS)
        out = []
        for part in range(2):
            near = extended[part, rows, pl.ds(left_base, width)].reshape(lane.shape)
            far = extended[part, rows, pl.ds(left_base + width, width)].reshape(lane.shape)
            value = pltpu.roll(jnp.where(lane < off, far, near), lax.rem(width - off, width), 2)
            value = pltpu.roll(value, lax.rem(ROWS - down, ROWS), 1)
            value = jnp.where(row < ROWS - down, value[:tiles], value[1:])
            out.append(value.reshape(width, width))
        return out

    def add(slot, terms):
        top_base, down, left_base, off = corner(slot)
        rows = pl.ds(top_base, width + ROWS)
        for part in range(2):
            value = pltpu.roll(terms[part].reshape(row.shape), down, 1)
            value = pltpu.roll(value, off, 2)
            upper = jnp.where(row >= down, value, 0.0)
            lower = jnp.where(row >= down, 0.0, value)
            edge = jnp.zeros((1, ROWS, width), jnp.float32)
            value = jnp.concatenate([upper, edge], axis=0) + jnp.concatenate([edge, lower], axis=0)
            near = jnp.where(lane < off, 0.0, value).reshape(width + ROWS, width)
            far = jnp.where(lane < off, value, 0.0).reshape(width + ROWS, width)
            gradient[part, rows, pl.ds(left_base, width)] += near
            gradient[part, rows, pl.ds(left_base + width, width)] += far

    def body(group, carry):
        pairs = [
            [group * GROUP + 2 * pair, group * GROUP + 2 * pair + 1] for pair in range(GROUP // 2)
        ]
        for pair in pairs:
            patches = [cut(slot) for slot in pair]
            probe_re, probe_im = probe[0], probe[1]
            waves = [
                (probe_re * re - probe_im * im, probe_re * im + probe_im * re) for re, im in patches
            ]
            far = right_apply(right_tables[0], left_apply(left_tables[0], waves))
            scaled = []
            for slot, (re, im) in zip(pair, far):
                filled = jnp.where(tops[slot] >= 0, 1.0, 0.0)
                misfit = (re * re + im * im - measured[slot]) * filled
                scaled.append((misfit * re, misfit * im))
            back = left_apply(left_tables[1], right_apply(right_tables[1], scaled))
            probe_terms = [
                (qr * br + qi * bi, qr * bi - qi * br) for (qr, qi), (br, bi) in zip(patches, back)
            ]
            probe_gradient[:width] += probe_terms[0][0] + probe_terms[1][0]
            probe_gradient[width:] += probe_terms[0][1] + probe_terms[1][1]
            for slot, (br, bi) in zip(pair, back):
                add(slot, (probe_re * br + probe_im * bi, probe_re * bi - probe_im * br))
        return carry

    lax.fori_loop(0, slots // GROUP, body, 0)


def run_step(tops, lefts, extended, probe, measured, tables):
    vmem = pl.BlockSpec(memory_space=pltpu.VMEM)
    smem = pl.BlockSpec(memory_space=pltpu.SMEM)
    width = probe.shape[1]
    slots = measured.shape[0]
    return pl.pallas_call(
        step_kernel,
        out_shape=(
            jax.ShapeDtypeStruct(extended.shape, jnp.float32),
            jax.ShapeDtypeStruct((2 * width, width), jnp.float32),
        ),
        in_specs=[smem, smem] + [vmem] * 5,
        out_specs=(vmem, vmem),
        compiler_params=pltpu.CompilerParams(vmem_limit_bytes=40 * 1024 * 1024),
        cost_estimate=pl.CostEstimate(
            flops=slots * 24 * 8 * width**3, bytes_accessed=8 * 1024 * 1024, transcendentals=0
        ),
    )(tops, lefts, extended, probe, measured, *tables)


def remote(source, target, send, receive, ty, tx):
    return pltpu.make_async_remote_copy(
        src_ref=source,
        dst_ref=target,
        send_sem=send,
        recv_sem=receive,
        device_id=(ty, tx),
        device_id_type=pl.DeviceIdType.MESH,
    )


def only(condition):
    return pl.when(condition)


def greet(partners):
    barrier = pltpu.get_barrier_semaphore()
    count = 0
    for exists, ty, tx in partners:

        def signal(ty=ty, tx=tx):
            pl.semaphore_signal(
                barrier, inc=1, device_id=(ty, tx), device_id_type=pl.DeviceIdType.MESH
            )

        if exists is True:
            signal()
            count = count + 1
        else:
            only(exists)(signal)
            count = count + exists.astype(jnp.int32)
    pl.semaphore_wait(barrier, count)


def peers(band_count, ty, tx):
    return [(True, lax.rem(ty + k, band_count), tx) for k in range(1, band_count)]


def stage_measured(step_number, intensities, holder, staged, outgoing, measured, load_sem, ty):
    load = pltpu.make_async_copy(intensities.at[step_number], staged, load_sem)
    load.start()
    load.wait()

    def place(slot, carry):
        outgoing[slot] = staged[holder[step_number, slot]]
        return carry

    lax.fori_loop(0, outgoing.shape[0], place, 0)
    for own in range(CAP):
        measured[ty * CAP + own] = staged[holder[step_number, ty * CAP + own]]


def measured_copies(band_count, outgoing, measured, send_sems, recv_sems, ty, tx):
    copies = []
    for k in range(1, band_count):
        peer = lax.rem(ty + k, band_count)
        copies.append(
            remote(
                outgoing.at[pl.ds(peer * CAP, CAP)],
                measured.at[pl.ds(ty * CAP, CAP)],
                send_sems.at[k - 1],
                recv_sems.at[k - 1],
                peer,
                tx,
            )
        )
    return copies


def begin_kernel(
    sizes, holder, intensities, object_field, wants, measured, extended, received,
    staged, outgoing, load_sem, own_sem, send_sems, recv_sems, want_send, want_recv, halo_send, halo_recv,
):
    band_count, strip_count, width = sizes
    ty, tx = lax.axis_index("ty"), lax.axis_index("tx")
    rows, cols = object_field.shape[1:]
    above, left = ty > 0, tx > 0
    below, right = ty < band_count - 1, tx < strip_count - 1
    own = pltpu.make_async_copy(object_field, extended.at[:, :rows, :cols], own_sem)
    own.start()
    greet(
        peers(band_count, ty, tx)
        + [
            (left, ty, tx - 1),
            (right, ty, tx + 1),
            (above & left, ty - 1, tx - 1),
            (below & right, ty + 1, tx + 1),
        ]
    )
    want_copies = []
    for k in range(1, band_count):
        peer = lax.rem(ty + k, band_count)
        want_copies.append(
            remote(wants.at[peer], received.at[ty], want_send.at[k - 1], want_recv.at[k - 1], peer, tx)
        )
    for copy in want_copies:
        copy.start()
    halos = [
        (
            left, right,
            remote(object_field.at[:, :, :width], extended.at[:, :rows, cols:],
                   halo_send.at[0], halo_recv.at[0], ty, tx - 1),
        ),
        (
            above, below,
            remote(object_field.at[:, :width, :], extended.at[:, rows:, :cols],
                   halo_send.at[1], halo_recv.at[1], ty - 1, tx),
        ),
        (
            above & left, below & right,
            remote(object_field.at[:, :width, :width], extended.at[:, rows:, cols:],
                   halo_send.at[2], halo_recv.at[2], ty - 1, tx - 1),
        ),
    ]
    for sends, _, copy in halos:
        only(sends)(copy.start)
    stage_measured(0, intensities, holder, staged, outgoing, measured, load_sem, ty)
    copies = measured_copies(band_count, outgoing, measured, send_sems, recv_sems, ty, tx)
    for copy in copies:
        copy.start()
    received[ty] = wants[ty]

    @only(jnp.logical_not(right))
    def _():
        extended[:, :rows, cols:] = jnp.zeros((2, rows, width), jnp.float32)

    @only(jnp.logical_not(below))
    def _():
        extended[:, rows:, :cols] = jnp.zeros((2, width, cols), jnp.float32)

    @only(jnp.logical_not(below & right))
    def _():
        extended[:, rows:, cols:] = jnp.zeros((2, width, width), jnp.float32)

    own.wait()
    for copy in want_copies:
        copy.wait()
    for sends, receives, copy in halos:
        only(sends)(copy.wait_send)
        only(receives)(copy.wait_recv)
    for copy in copies:
        copy.wait()


def strip_peers(strip_count, ty, tx):
    return [(True, ty, lax.rem(tx + k, strip_count)) for k in range(1, strip_count)]


class ProbeSum:
    def __init__(self, sizes, probe_term, total, band_parts, strip_parts, band_sems, strip_sems, share_sems, ty, tx):
        band_count, strip_count, _ = sizes
        self.ty, self.tx = ty, tx
        self.probe_term, self.total = probe_term, total
        self.band_parts, self.strip_parts = band_parts, strip_parts
        rows = total.shape[0] // band_count
        self.mine = pl.ds(ty * rows, rows)
        self.to_bands, self.to_strips, self.shares = [], [], []
        for k in range(1, band_count):
            peer = lax.rem(ty + k, band_count)
            self.to_bands.append(
                remote(probe_term.at[pl.ds(peer * rows, rows)], band_parts.at[k - 1],
                       band_sems.at[0, k - 1], band_sems.at[1, k - 1], peer, tx)
            )
            self.shares.append(
                remote(total.at[self.mine], total.at[self.mine],
                       share_sems.at[0, k - 1], share_sems.at[1, k - 1], peer, tx)
            )
        for k in range(1, strip_count):
            peer = lax.rem(tx + k, strip_count)
            self.to_strips.append(
                remote(strip_parts.at[tx], strip_parts.at[tx],
                       strip_sems.at[0, k - 1], strip_sems.at[1, k - 1], ty, peer)
            )

    def start(self):
        for copy in self.to_bands:
            copy.start()

    def over_strips(self):
        for copy in self.to_bands:
            copy.wait()
        value = self.probe_term[self.mine, :]
        for k in range(self.band_parts.shape[0]):
            value = value + self.band_parts[k]
        self.strip_parts[self.tx] = value
        for copy in self.to_strips:
            copy.start()

    def share(self):
        for copy in self.to_strips:
            copy.wait()
        value = self.strip_parts[0]
        for k in range(1, self.strip_parts.shape[0]):
            value = value + self.strip_parts[k]
        self.total[self.mine, :] = value
        for copy in self.shares:
            copy.start()

    def finish(self, scale, probe, new_probe):
        for copy in self.shares:
            copy.wait()
        width = probe.shape[1]
        for part in range(2):
            new_probe[part] = probe[part] - scale * self.total[part * width : (part + 1) * width]


def middle_kernel(
    sizes, scale, holder, intensities, gradient, probe_term, extended, probe, measured, new_extended, new_probe,
    staged, outgoing, load_sem, send_sems, recv_sems, side, ends, ends_out, side_send, side_recv, end_send, end_recv,
    total, band_parts, strip_parts, band_sems, strip_sems, share_sems,
):
    band_count, strip_count, width = sizes
    ty, tx = lax.axis_index("ty"), lax.axis_index("tx")
    rows, cols = (size - width for size in extended.shape[1:])
    above, left = ty > 0, tx > 0
    below, right = ty < band_count - 1, tx < strip_count - 1
    greet(
        peers(band_count, ty, tx)
        + strip_peers(strip_count, ty, tx)
    )
    probe_sum = ProbeSum(
        sizes, probe_term, total, band_parts, strip_parts, band_sems, strip_sems, share_sems, ty, tx
    )
    probe_sum.start()
    sides = [
        (right, left, remote(gradient.at[:, :, cols:], side.at[0], side_send.at[0], side_recv.at[0], ty, tx + 1)),
        (left, right, remote(gradient.at[:, :, :width], side.at[1], side_send.at[1], side_recv.at[1], ty, tx - 1)),
    ]
    stage_measured(1, intensities, holder, staged, outgoing, measured, load_sem, ty)
    probe_sum.over_strips()
    for sends, _, copy in sides:
        only(sends)(copy.start)
    probe_sum.share()
    measured_sends = measured_copies(band_count, outgoing, measured, send_sems, recv_sems, ty, tx)
    for copy in measured_sends:
        copy.start()
    for number, (_, receives, _) in enumerate(sides):

        @only(jnp.logical_not(receives))
        def _(number=number):
            side[number] = jnp.zeros(side.shape[1:], jnp.float32)

    for sends, receives, copy in sides:
        only(sends)(copy.wait_send)
        only(receives)(copy.wait_recv)
    for number, first in enumerate((rows, 0)):
        block = pl.ds(first, width)
        ends_out[number, :, :, :width] = gradient[:, block, :width] + side[0, :, block, :]
        ends_out[number, :, :, width:cols] = gradient[:, block, width:cols]
        ends_out[number, :, :, cols:] = gradient[:, block, cols:] + side[1, :, block, :]
    end_copies = [
        (below, above, remote(ends_out.at[0], ends.at[0], end_send.at[0], end_recv.at[0], ty + 1, tx)),
        (above, below, remote(ends_out.at[1], ends.at[1], end_send.at[1], end_recv.at[1], ty - 1, tx)),
    ]
    for sends, _, copy in end_copies:
        only(sends)(copy.start)
    for number, (_, receives, _) in enumerate(end_copies):

        @only(jnp.logical_not(receives))
        def _(number=number):
            ends[number] = jnp.zeros(ends.shape[1:], jnp.float32)

    inner = pl.ds(width, rows - width)
    new_extended[:, inner, :width] = extended[:, inner, :width] - OBJECT_RATE * (
        gradient[:, inner, :width] + side[0, :, inner, :]
    )
    new_extended[:, inner, width:cols] = (
        extended[:, inner, width:cols] - OBJECT_RATE * gradient[:, inner, width:cols]
    )
    new_extended[:, inner, cols:] = extended[:, inner, cols:] - OBJECT_RATE * (
        gradient[:, inner, cols:] + side[1, :, inner, :]
    )
    for sends, receives, copy in end_copies:
        only(sends)(copy.wait_send)
        only(receives)(copy.wait_recv)
    new_extended[:, :width, :] = extended[:, :width, :] - OBJECT_RATE * (ends_out[1] + ends[0])
    new_extended[:, rows:, :] = extended[:, rows:, :] - OBJECT_RATE * (ends_out[0] + ends[1])
    probe_sum.finish(scale, probe, new_probe)
    for copy in measured_sends:
        copy.wait()


def end_kernel(
    sizes, scale, gradient, probe_term, extended, probe, new_object, new_probe,
    side, end, corner, halo_send, halo_recv,
    total, band_parts, strip_parts, band_sems, strip_sems, share_sems,
):
    band_count, strip_count, width = sizes
    ty, tx = lax.axis_index("ty"), lax.axis_index("tx")
    rows, cols = new_object.shape[1:]
    above, left = ty > 0, tx > 0
    below, right = ty < band_count - 1, tx < strip_count - 1
    greet(
        peers(band_count, ty, tx)
        + strip_peers(strip_count, ty, tx)
        + [(above & left, ty - 1, tx - 1), (below & right, ty + 1, tx + 1)]
    )
    probe_sum = ProbeSum(
        sizes, probe_term, total, band_parts, strip_parts, band_sems, strip_sems, share_sems, ty, tx
    )
    probe_sum.start()
    halos = [
        (right, left, side, remote(gradient.at[:, :rows, cols:], side, halo_send.at[0], halo_recv.at[0], ty, tx + 1)),
        (below, above, end, remote(gradient.at[:, rows:, :cols], end, halo_send.at[1], halo_recv.at[1], ty + 1, tx)),
        (
            below & right, above & left, corner,
            remote(gradient.at[:, rows:, cols:], corner, halo_send.at[2], halo_recv.at[2], ty + 1, tx + 1),
        ),
    ]
    only(halos[1][0])(halos[1][3].start)
    probe_sum.over_strips()
    only(halos[0][0])(halos[0][3].start)
    only(halos[2][0])(halos[2][3].start)
    probe_sum.share()
    for _, receives, target, _ in halos:

        @only(jnp.logical_not(receives))
        def _(target=target):
            target[...] = jnp.zeros(target.shape, jnp.float32)

    new_object[:, width:, width:] = (
        extended[:, width:rows, width:cols] - OBJECT_RATE * gradient[:, width:rows, width:cols]
    )
    probe_sum.finish(scale, probe, new_probe)
    for sends, receives, _, copy in halos:
        only(sends)(copy.wait_send)
        only(receives)(copy.wait_recv)
    new_object[:, width:, :width] = extended[:, width:rows, :width] - OBJECT_RATE * (
        gradient[:, width:rows, :width] + side[:, width:, :]
    )
    new_object[:, :width, width:] = extended[:, :width, width:cols] - OBJECT_RATE * (
        gradient[:, :width, width:cols] + end[:, :, width:]
    )
    new_object[:, :width, :width] = extended[:, :width, :width] - OBJECT_RATE * (
        gradient[:, :width, :width] + side[:, :width, :] + end[:, :, :width] + corner[...]
    )


VMEM = pl.BlockSpec(memory_space=pltpu.VMEM)
SMEM = pl.BlockSpec(memory_space=pltpu.SMEM)
HBM = pl.BlockSpec(memory_space=pl.ANY)
DMA = pltpu.SemaphoreType.DMA


def floats(*shape):
    return jax.ShapeDtypeStruct(shape, jnp.float32)


def communicate(kernel, number, in_specs, shapes, scratch):
    return pl.pallas_call(
        kernel,
        out_shape=shapes,
        in_specs=in_specs,
        out_specs=tuple(VMEM for _ in shapes),
        scratch_shapes=scratch,
        compiler_params=pltpu.CompilerParams(
            collective_id=number, has_side_effects=True, vmem_limit_bytes=48 * 1024 * 1024
        ),
    )


def on_device(object_field, probe_field, owners, row_offsets, col_offsets, intensities):
    band_count = lax.axis_size("ty")
    strip_count = lax.axis_size("tx")
    tile_rows = object_field.shape[1]
    tile_cols = object_field.shape[2]
    width = probe_field.shape[1]
    batch_rows = row_offsets.shape[1]
    slot_count = band_count * CAP
    strip_index = lax.axis_index("tx")
    tables = [jnp.asarray(table) for table in dft_tables(width)]
    probe_scale = PROBE_RATE / (batch_rows * band_count * strip_count)

    owner_rows = owners[:, :, 0]
    position_ids = jnp.arange(batch_rows, dtype=jnp.int32)
    earlier = (owner_rows[:, None, :] == owner_rows[:, :, None]) & (
        position_ids[None, None, :] < position_ids[None, :, None]
    )
    slot_of = owner_rows * CAP + jnp.sum(earlier.astype(jnp.int32), axis=2)
    top_local = (
        jnp.minimum(owner_rows * tile_rows + row_offsets, tile_rows * band_count - width)
        - owner_rows * tile_rows
    )
    left_local = (
        jnp.minimum(strip_index * tile_cols + col_offsets, tile_cols * strip_count - width)
        - strip_index * tile_cols
    )
    slot_ids = jnp.arange(slot_count, dtype=jnp.int32)
    matches = slot_of[:, None, :] == slot_ids[None, :, None]
    filled = jnp.any(matches, axis=2)

    def by_slot(values):
        return jnp.sum(jnp.where(matches, values[:, None, :], 0), axis=2)

    want_top = jnp.where(filled, by_slot(top_local), -1)
    want_left = by_slot(left_local)
    holder = by_slot(jnp.broadcast_to(position_ids[None], slot_of.shape))
    sizes = (band_count, strip_count, width)
    wants = jnp.concatenate([want_top, want_left]).reshape(2 * STEPS, band_count, CAP).transpose(1, 0, 2)
    wants = jnp.pad(wants, ((0, 0), (0, 8 - 2 * STEPS), (0, 128 - CAP)))
    staging = [
        pltpu.VMEM((batch_rows, width, width), jnp.float32),
        pltpu.VMEM((slot_count, width, width), jnp.float32),
        DMA,
    ]
    pair_sems = [DMA((band_count - 1,)), DMA((band_count - 1,))]
    measured, extended, received = communicate(
        functools.partial(begin_kernel, sizes),
        0,
        [SMEM, HBM, HBM, VMEM],
        (
            floats(slot_count, width, width),
            floats(2, tile_rows + width, tile_cols + width),
            jax.ShapeDtypeStruct(wants.shape, jnp.int32),
        ),
        staging + [DMA] + pair_sems + pair_sems + [DMA((3,)), DMA((3,))],
    )(holder, intensities, object_field, wants)
    received = received[:, : 2 * STEPS, :CAP].transpose(1, 0, 2).reshape(2, STEPS, slot_count)
    share_rows = 2 * width // band_count
    summing = [
        pltpu.VMEM((2 * width, width), jnp.float32),
        pltpu.VMEM((band_count - 1, share_rows, width), jnp.float32),
        pltpu.VMEM((strip_count, share_rows, width), jnp.float32),
        DMA((2, band_count - 1)),
        DMA((2, strip_count - 1)),
        DMA((2, band_count - 1)),
    ]
    gradient, probe_term = run_step(received[0, 0], received[1, 0], extended, probe_field, measured, tables)
    measured, extended, probe_field = communicate(
        functools.partial(middle_kernel, sizes, probe_scale),
        1,
        [SMEM, HBM] + [VMEM] * 4,
        (floats(*measured.shape), floats(*extended.shape), floats(*probe_field.shape)),
        staging
        + pair_sems
        + [
            pltpu.VMEM((2, 2, tile_rows + width, width), jnp.float32),
            pltpu.VMEM((2, 2, width, tile_cols + width), jnp.float32),
            pltpu.VMEM((2, 2, width, tile_cols + width), jnp.float32),
        ]
        + [DMA((2,))] * 4
        + summing,
    )(holder, intensities, gradient, probe_term, extended, probe_field)
    gradient, probe_term = run_step(received[0, 1], received[1, 1], extended, probe_field, measured, tables)
    return communicate(
        functools.partial(end_kernel, sizes, probe_scale),
        2,
        [VMEM] * 4,
        (floats(*object_field.shape), floats(*probe_field.shape)),
        [
            pltpu.VMEM((2, tile_rows, width), jnp.float32),
            pltpu.VMEM((2, width, tile_cols), jnp.float32),
            pltpu.VMEM((2, width, width), jnp.float32),
            DMA((3,)),
            DMA((3,)),
        ]
        + summing,
    )(gradient, probe_term, extended, probe_field)


def solution(mesh):
    in_specs = (
        P(None, "ty", "tx"),
        P(),
        P(None, ("ty", "tx"), None),
        P(None, ("ty", "tx")),
        P(None, ("ty", "tx")),
        P(None, ("ty", "tx"), None, None),
    )
    out_specs = (P(None, "ty", "tx"), P())
    return jax.shard_map(
        on_device, mesh=mesh, in_specs=in_specs, out_specs=out_specs, check_vma=False
    )
```

```python
import functools
import math

import jax
import jax.numpy as jnp
import ml_dtypes
import numpy as np
from jax import lax
from jax.experimental import pallas as pl
from jax.experimental.pallas import tpu as pltpu
from jax.sharding import PartitionSpec as P

CAP = 3
STEPS = 2
GROUP = 8
JOINT = 8
ROWS = 8

OBJECT_RATE = 0.25
PROBE_RATE = 1.0


def split_table(table):
    high = table.astype(ml_dtypes.bfloat16)
    low = (table - high.astype(np.float64)).astype(ml_dtypes.bfloat16)
    return high, low


def dft_tables(width):
    counter = np.arange(width)
    radians = (counter[:, None] * counter[None, :] % width) * (2.0 * math.pi / width)
    cos = np.cos(radians) / math.sqrt(width)
    sin = -np.sin(radians) / math.sqrt(width)
    plus = np.block([[cos, -sin], [sin, cos]])
    minus = np.block([[cos, sin], [-sin, cos]])

    def left(table):
        high, low = split_table(table)
        return np.concatenate([high, low, high], axis=1)

    def right(table):
        high, low = split_table(table)
        return np.concatenate([high, low, high], axis=0)

    return np.stack([left(plus), left(minus)]), np.stack([right(minus), right(plus)])


def split(value):
    high = value.astype(jnp.bfloat16)
    low = (value - high.astype(jnp.float32)).astype(jnp.bfloat16)
    return high, low


def left_apply(table, parts):
    data = jnp.concatenate(
        [jnp.concatenate([re for re, _ in parts], axis=1), jnp.concatenate([im for _, im in parts], axis=1)],
        axis=0,
    )
    high, low = split(data)
    out = jnp.dot(table, jnp.concatenate([high, high, low], axis=0), preferred_element_type=jnp.float32)
    width = out.shape[0] // 2
    return [
        (out[:width, i * width : (i + 1) * width], out[width:, i * width : (i + 1) * width])
        for i in range(len(parts))
    ]


def right_apply(table, parts):
    data = jnp.concatenate([jnp.concatenate([re, im], axis=1) for re, im in parts], axis=0)
    high, low = split(data)
    out = jnp.dot(jnp.concatenate([high, high, low], axis=1), table, preferred_element_type=jnp.float32)
    width = out.shape[1] // 2
    return [
        (out[i * width : (i + 1) * width, :width], out[i * width : (i + 1) * width, width:])
        for i in range(len(parts))
    ]


def step_kernel(
    tops, lefts, extended, probe, measured, left_tables, right_tables, gradient, probe_gradient
):
    width = probe.shape[1]
    slots = measured.shape[0]
    gradient[...] = jnp.zeros_like(gradient)
    probe_gradient[...] = jnp.zeros_like(probe_gradient)
    tiles = width // ROWS
    lane = lax.broadcasted_iota(jnp.int32, (tiles + 1, ROWS, width), 2)
    row = lax.broadcasted_iota(jnp.int32, (tiles, ROWS, width), 1)

    def corner(slot):
        top = jnp.maximum(tops[slot], 0)
        left = lefts[slot]
        top_base = pl.multiple_of(top // ROWS * ROWS, ROWS)
        left_base = pl.multiple_of(left // width * width, width)
        return top_base, top - top_base, left_base, left - left_base

    def cut(slot):
        top_base, down, left_base, off = corner(slot)
        rows = pl.ds(top_base, width + ROWS)
        out = []
        for part in range(2):
            near = extended[part, rows, pl.ds(left_base, width)].reshape(lane.shape)
            far = extended[part, rows, pl.ds(left_base + width, width)].reshape(lane.shape)
            value = pltpu.roll(jnp.where(lane < off, far, near), lax.rem(width - off, width), 2)
            value = pltpu.roll(value, lax.rem(ROWS - down, ROWS), 1)
            value = jnp.where(row < ROWS - down, value[:tiles], value[1:])
            out.append(value.reshape(width, width))
        return out

    def add(slot, terms):
        top_base, down, left_base, off = corner(slot)
        rows = pl.ds(top_base, width + ROWS)
        for part in range(2):
            value = pltpu.roll(terms[part].reshape(row.shape), down, 1)
            value = pltpu.roll(value, off, 2)
            upper = jnp.where(row >= down, value, 0.0)
            lower = jnp.where(row >= down, 0.0, value)
            edge = jnp.zeros((1, ROWS, width), jnp.float32)
            value = jnp.concatenate([upper, edge], axis=0) + jnp.concatenate([edge, lower], axis=0)
            near = jnp.where(lane < off, 0.0, value).reshape(width + ROWS, width)
            far = jnp.where(lane < off, value, 0.0).reshape(width + ROWS, width)
            gradient[part, rows, pl.ds(left_base, width)] += near
            gradient[part, rows, pl.ds(left_base + width, width)] += far

    def body(group, carry):
        pairs = [
            [group * GROUP + JOINT * pair + i for i in range(JOINT)] for pair in range(GROUP // JOINT)
        ]
        for pair in pairs:
            patches = [cut(slot) for slot in pair]
            probe_re, probe_im = probe[0], probe[1]
            waves = [
                (probe_re * re - probe_im * im, probe_re * im + probe_im * re) for re, im in patches
            ]
            far = right_apply(right_tables[0], left_apply(left_tables[0], waves))
            scaled = []
            for slot, (re, im) in zip(pair, far):
                filled = jnp.where(tops[slot] >= 0, 1.0, 0.0)
                misfit = (re * re + im * im - measured[slot]) * filled
                scaled.append((misfit * re, misfit * im))
            back = left_apply(left_tables[1], right_apply(right_tables[1], scaled))
            probe_terms = [
                (qr * br + qi * bi, qr * bi - qi * br) for (qr, qi), (br, bi) in zip(patches, back)
            ]
            probe_gradient[:width] += sum(re for re, _ in probe_terms)
            probe_gradient[width:] += sum(im for _, im in probe_terms)
            for slot, (br, bi) in zip(pair, back):
                add(slot, (probe_re * br + probe_im * bi, probe_re * bi - probe_im * br))
        return carry

    lax.fori_loop(0, slots // GROUP, body, 0)


def run_step(tops, lefts, extended, probe, measured, tables):
    vmem = pl.BlockSpec(memory_space=pltpu.VMEM)
    smem = pl.BlockSpec(memory_space=pltpu.SMEM)
    width = probe.shape[1]
    slots = measured.shape[0]
    return pl.pallas_call(
        step_kernel,
        out_shape=(
            jax.ShapeDtypeStruct(extended.shape, jnp.float32),
            jax.ShapeDtypeStruct((2 * width, width), jnp.float32),
        ),
        in_specs=[smem, smem] + [vmem] * 5,
        out_specs=(vmem, vmem),
        compiler_params=pltpu.CompilerParams(vmem_limit_bytes=40 * 1024 * 1024),
        cost_estimate=pl.CostEstimate(
            flops=slots * 24 * 8 * width**3, bytes_accessed=8 * 1024 * 1024, transcendentals=0
        ),
    )(tops, lefts, extended, probe, measured, *tables)


def remote(source, target, send, receive, ty, tx):
    return pltpu.make_async_remote_copy(
        src_ref=source,
        dst_ref=target,
        send_sem=send,
        recv_sem=receive,
        device_id=(ty, tx),
        device_id_type=pl.DeviceIdType.MESH,
    )


def only(condition):
    return pl.when(condition)


def greet(partners):
    barrier = pltpu.get_barrier_semaphore()
    count = 0
    for exists, ty, tx in partners:

        def signal(ty=ty, tx=tx):
            pl.semaphore_signal(
                barrier, inc=1, device_id=(ty, tx), device_id_type=pl.DeviceIdType.MESH
            )

        if exists is True:
            signal()
            count = count + 1
        else:
            only(exists)(signal)
            count = count + exists.astype(jnp.int32)
    pl.semaphore_wait(barrier, count)


def peers(band_count, ty, tx):
    return [(True, lax.rem(ty + k, band_count), tx) for k in range(1, band_count)]


def stage_measured(step_number, intensities, holder, staged, outgoing, measured, load_sem, ty):
    load = pltpu.make_async_copy(intensities.at[step_number], staged, load_sem)
    load.start()
    load.wait()

    def place(slot, carry):
        outgoing[slot] = staged[holder[step_number, slot]]
        return carry

    lax.fori_loop(0, outgoing.shape[0], place, 0)
    for own in range(CAP):
        measured[ty * CAP + own] = staged[holder[step_number, ty * CAP + own]]


def measured_copies(band_count, outgoing, measured, send_sems, recv_sems, ty, tx):
    copies = []
    for k in range(1, band_count):
        peer = lax.rem(ty + k, band_count)
        copies.append(
            remote(
                outgoing.at[pl.ds(peer * CAP, CAP)],
                measured.at[pl.ds(ty * CAP, CAP)],
                send_sems.at[k - 1],
                recv_sems.at[k - 1],
                peer,
                tx,
            )
        )
    return copies


def begin_kernel(
    sizes, holder, intensities, object_field, wants, measured, extended, received,
    staged, outgoing, load_sem, own_sem, send_sems, recv_sems, want_send, want_recv, halo_send, halo_recv,
):
    band_count, strip_count, width = sizes
    ty, tx = lax.axis_index("ty"), lax.axis_index("tx")
    rows, cols = object_field.shape[1:]
    above, left = ty > 0, tx > 0
    below, right = ty < band_count - 1, tx < strip_count - 1
    own = pltpu.make_async_copy(object_field, extended.at[:, :rows, :cols], own_sem)
    own.start()
    greet(
        peers(band_count, ty, tx)
        + [
            (left, ty, tx - 1),
            (right, ty, tx + 1),
            (above & left, ty - 1, tx - 1),
            (below & right, ty + 1, tx + 1),
        ]
    )
    want_copies = []
    for k in range(1, band_count):
        peer = lax.rem(ty + k, band_count)
        want_copies.append(
            remote(wants.at[peer], received.at[ty], want_send.at[k - 1], want_recv.at[k - 1], peer, tx)
        )
    for copy in want_copies:
        copy.start()
    halos = [
        (
            left, right,
            remote(object_field.at[:, :, :width], extended.at[:, :rows, cols:],
                   halo_send.at[0], halo_recv.at[0], ty, tx - 1),
        ),
        (
            above, below,
            remote(object_field.at[:, :width, :], extended.at[:, rows:, :cols],
                   halo_send.at[1], halo_recv.at[1], ty - 1, tx),
        ),
        (
            above & left, below & right,
            remote(object_field.at[:, :width, :width], extended.at[:, rows:, cols:],
                   halo_send.at[2], halo_recv.at[2], ty - 1, tx - 1),
        ),
    ]
    for sends, _, copy in halos:
        only(sends)(copy.start)
    stage_measured(0, intensities, holder, staged, outgoing, measured, load_sem, ty)
    copies = measured_copies(band_count, outgoing, measured, send_sems, recv_sems, ty, tx)
    for copy in copies:
        copy.start()
    received[ty] = wants[ty]

    @only(jnp.logical_not(right))
    def _():
        extended[:, :rows, cols:] = jnp.zeros((2, rows, width), jnp.float32)

    @only(jnp.logical_not(below))
    def _():
        extended[:, rows:, :cols] = jnp.zeros((2, width, cols), jnp.float32)

    @only(jnp.logical_not(below & right))
    def _():
        extended[:, rows:, cols:] = jnp.zeros((2, width, width), jnp.float32)

    own.wait()
    for copy in want_copies:
        copy.wait()
    for sends, receives, copy in halos:
        only(sends)(copy.wait_send)
        only(receives)(copy.wait_recv)
    for copy in copies:
        copy.wait()


def strip_peers(strip_count, ty, tx):
    return [(True, ty, lax.rem(tx + k, strip_count)) for k in range(1, strip_count)]


class ProbeSum:
    def __init__(self, sizes, probe_term, total, band_parts, strip_parts, band_sems, strip_sems, share_sems, ty, tx):
        band_count, strip_count, _ = sizes
        self.ty, self.tx = ty, tx
        self.probe_term, self.total = probe_term, total
        self.band_parts, self.strip_parts = band_parts, strip_parts
        rows = total.shape[0] // band_count
        self.mine = pl.ds(ty * rows, rows)
        self.to_bands, self.to_strips, self.shares = [], [], []
        for k in range(1, band_count):
            peer = lax.rem(ty + k, band_count)
            self.to_bands.append(
                remote(probe_term.at[pl.ds(peer * rows, rows)], band_parts.at[k - 1],
                       band_sems.at[0, k - 1], band_sems.at[1, k - 1], peer, tx)
            )
            self.shares.append(
                remote(total.at[self.mine], total.at[self.mine],
                       share_sems.at[0, k - 1], share_sems.at[1, k - 1], peer, tx)
            )
        for k in range(1, strip_count):
            peer = lax.rem(tx + k, strip_count)
            self.to_strips.append(
                remote(strip_parts.at[tx], strip_parts.at[tx],
                       strip_sems.at[0, k - 1], strip_sems.at[1, k - 1], ty, peer)
            )

    def start(self):
        for copy in self.to_bands:
            copy.start()

    def over_strips(self):
        for copy in self.to_bands:
            copy.wait()
        value = self.probe_term[self.mine, :]
        for k in range(self.band_parts.shape[0]):
            value = value + self.band_parts[k]
        self.strip_parts[self.tx] = value
        for copy in self.to_strips:
            copy.start()

    def share(self):
        for copy in self.to_strips:
            copy.wait()
        value = self.strip_parts[0]
        for k in range(1, self.strip_parts.shape[0]):
            value = value + self.strip_parts[k]
        self.total[self.mine, :] = value
        for copy in self.shares:
            copy.start()

    def finish(self, scale, probe, new_probe):
        for copy in self.shares:
            copy.wait()
        width = probe.shape[1]
        for part in range(2):
            new_probe[part] = probe[part] - scale * self.total[part * width : (part + 1) * width]


def middle_kernel(
    sizes, scale, holder, intensities, gradient, probe_term, extended, probe, measured, new_extended, new_probe,
    staged, outgoing, load_sem, send_sems, recv_sems, side, ends, ends_out, side_send, side_recv, end_send, end_recv,
    total, band_parts, strip_parts, band_sems, strip_sems, share_sems,
):
    band_count, strip_count, width = sizes
    ty, tx = lax.axis_index("ty"), lax.axis_index("tx")
    rows, cols = (size - width for size in extended.shape[1:])
    above, left = ty > 0, tx > 0
    below, right = ty < band_count - 1, tx < strip_count - 1
    greet(
        peers(band_count, ty, tx)
        + strip_peers(strip_count, ty, tx)
    )
    probe_sum = ProbeSum(
        sizes, probe_term, total, band_parts, strip_parts, band_sems, strip_sems, share_sems, ty, tx
    )
    probe_sum.start()
    sides = [
        (right, left, remote(gradient.at[:, :, cols:], side.at[0], side_send.at[0], side_recv.at[0], ty, tx + 1)),
        (left, right, remote(gradient.at[:, :, :width], side.at[1], side_send.at[1], side_recv.at[1], ty, tx - 1)),
    ]
    stage_measured(1, intensities, holder, staged, outgoing, measured, load_sem, ty)
    probe_sum.over_strips()
    for sends, _, copy in sides:
        only(sends)(copy.start)
    probe_sum.share()
    measured_sends = measured_copies(band_count, outgoing, measured, send_sems, recv_sems, ty, tx)
    for copy in measured_sends:
        copy.start()
    for number, (_, receives, _) in enumerate(sides):

        @only(jnp.logical_not(receives))
        def _(number=number):
            side[number] = jnp.zeros(side.shape[1:], jnp.float32)

    for sends, receives, copy in sides:
        only(sends)(copy.wait_send)
        only(receives)(copy.wait_recv)
    for number, first in enumerate((rows, 0)):
        block = pl.ds(first, width)
        ends_out[number, :, :, :width] = gradient[:, block, :width] + side[0, :, block, :]
        ends_out[number, :, :, width:cols] = gradient[:, block, width:cols]
        ends_out[number, :, :, cols:] = gradient[:, block, cols:] + side[1, :, block, :]
    end_copies = [
        (below, above, remote(ends_out.at[0], ends.at[0], end_send.at[0], end_recv.at[0], ty + 1, tx)),
        (above, below, remote(ends_out.at[1], ends.at[1], end_send.at[1], end_recv.at[1], ty - 1, tx)),
    ]
    for sends, _, copy in end_copies:
        only(sends)(copy.start)
    for number, (_, receives, _) in enumerate(end_copies):

        @only(jnp.logical_not(receives))
        def _(number=number):
            ends[number] = jnp.zeros(ends.shape[1:], jnp.float32)

    inner = pl.ds(width, rows - width)
    new_extended[:, inner, :width] = extended[:, inner, :width] - OBJECT_RATE * (
        gradient[:, inner, :width] + side[0, :, inner, :]
    )
    new_extended[:, inner, width:cols] = (
        extended[:, inner, width:cols] - OBJECT_RATE * gradient[:, inner, width:cols]
    )
    new_extended[:, inner, cols:] = extended[:, inner, cols:] - OBJECT_RATE * (
        gradient[:, inner, cols:] + side[1, :, inner, :]
    )
    for sends, receives, copy in end_copies:
        only(sends)(copy.wait_send)
        only(receives)(copy.wait_recv)
    new_extended[:, :width, :] = extended[:, :width, :] - OBJECT_RATE * (ends_out[1] + ends[0])
    new_extended[:, rows:, :] = extended[:, rows:, :] - OBJECT_RATE * (ends_out[0] + ends[1])
    probe_sum.finish(scale, probe, new_probe)
    for copy in measured_sends:
        copy.wait()


def end_kernel(
    sizes, scale, gradient, probe_term, extended, probe, new_object, new_probe,
    side, end, corner, halo_send, halo_recv,
    total, band_parts, strip_parts, band_sems, strip_sems, share_sems,
):
    band_count, strip_count, width = sizes
    ty, tx = lax.axis_index("ty"), lax.axis_index("tx")
    rows, cols = new_object.shape[1:]
    above, left = ty > 0, tx > 0
    below, right = ty < band_count - 1, tx < strip_count - 1
    greet(
        peers(band_count, ty, tx)
        + strip_peers(strip_count, ty, tx)
        + [(above & left, ty - 1, tx - 1), (below & right, ty + 1, tx + 1)]
    )
    probe_sum = ProbeSum(
        sizes, probe_term, total, band_parts, strip_parts, band_sems, strip_sems, share_sems, ty, tx
    )
    probe_sum.start()
    halos = [
        (right, left, side, remote(gradient.at[:, :rows, cols:], side, halo_send.at[0], halo_recv.at[0], ty, tx + 1)),
        (below, above, end, remote(gradient.at[:, rows:, :cols], end, halo_send.at[1], halo_recv.at[1], ty + 1, tx)),
        (
            below & right, above & left, corner,
            remote(gradient.at[:, rows:, cols:], corner, halo_send.at[2], halo_recv.at[2], ty + 1, tx + 1),
        ),
    ]
    only(halos[1][0])(halos[1][3].start)
    probe_sum.over_strips()
    only(halos[0][0])(halos[0][3].start)
    only(halos[2][0])(halos[2][3].start)
    probe_sum.share()
    for _, receives, target, _ in halos:

        @only(jnp.logical_not(receives))
        def _(target=target):
            target[...] = jnp.zeros(target.shape, jnp.float32)

    new_object[:, width:, width:] = (
        extended[:, width:rows, width:cols] - OBJECT_RATE * gradient[:, width:rows, width:cols]
    )
    probe_sum.finish(scale, probe, new_probe)
    for sends, receives, _, copy in halos:
        only(sends)(copy.wait_send)
        only(receives)(copy.wait_recv)
    new_object[:, width:, :width] = extended[:, width:rows, :width] - OBJECT_RATE * (
        gradient[:, width:rows, :width] + side[:, width:, :]
    )
    new_object[:, :width, width:] = extended[:, :width, width:cols] - OBJECT_RATE * (
        gradient[:, :width, width:cols] + end[:, :, width:]
    )
    new_object[:, :width, :width] = extended[:, :width, :width] - OBJECT_RATE * (
        gradient[:, :width, :width] + side[:, :width, :] + end[:, :, :width] + corner[...]
    )


VMEM = pl.BlockSpec(memory_space=pltpu.VMEM)
SMEM = pl.BlockSpec(memory_space=pltpu.SMEM)
HBM = pl.BlockSpec(memory_space=pl.ANY)
DMA = pltpu.SemaphoreType.DMA


def floats(*shape):
    return jax.ShapeDtypeStruct(shape, jnp.float32)


def communicate(kernel, number, in_specs, shapes, scratch):
    return pl.pallas_call(
        kernel,
        out_shape=shapes,
        in_specs=in_specs,
        out_specs=tuple(VMEM for _ in shapes),
        scratch_shapes=scratch,
        compiler_params=pltpu.CompilerParams(
            collective_id=number, has_side_effects=True, vmem_limit_bytes=48 * 1024 * 1024
        ),
    )


def on_device(object_field, probe_field, owners, row_offsets, col_offsets, intensities):
    band_count = lax.axis_size("ty")
    strip_count = lax.axis_size("tx")
    tile_rows = object_field.shape[1]
    tile_cols = object_field.shape[2]
    width = probe_field.shape[1]
    batch_rows = row_offsets.shape[1]
    slot_count = band_count * CAP
    strip_index = lax.axis_index("tx")
    tables = [jnp.asarray(table) for table in dft_tables(width)]
    probe_scale = PROBE_RATE / (batch_rows * band_count * strip_count)

    owner_rows = owners[:, :, 0]
    position_ids = jnp.arange(batch_rows, dtype=jnp.int32)
    earlier = (owner_rows[:, None, :] == owner_rows[:, :, None]) & (
        position_ids[None, None, :] < position_ids[None, :, None]
    )
    slot_of = owner_rows * CAP + jnp.sum(earlier.astype(jnp.int32), axis=2)
    top_local = (
        jnp.minimum(owner_rows * tile_rows + row_offsets, tile_rows * band_count - width)
        - owner_rows * tile_rows
    )
    left_local = (
        jnp.minimum(strip_index * tile_cols + col_offsets, tile_cols * strip_count - width)
        - strip_index * tile_cols
    )
    slot_ids = jnp.arange(slot_count, dtype=jnp.int32)
    matches = slot_of[:, None, :] == slot_ids[None, :, None]
    filled = jnp.any(matches, axis=2)

    def by_slot(values):
        return jnp.sum(jnp.where(matches, values[:, None, :], 0), axis=2)

    want_top = jnp.where(filled, by_slot(top_local), -1)
    want_left = by_slot(left_local)
    holder = by_slot(jnp.broadcast_to(position_ids[None], slot_of.shape))
    sizes = (band_count, strip_count, width)
    wants = jnp.concatenate([want_top, want_left]).reshape(2 * STEPS, band_count, CAP).transpose(1, 0, 2)
    wants = jnp.pad(wants, ((0, 0), (0, 8 - 2 * STEPS), (0, 128 - CAP)))
    staging = [
        pltpu.VMEM((batch_rows, width, width), jnp.float32),
        pltpu.VMEM((slot_count, width, width), jnp.float32),
        DMA,
    ]
    pair_sems = [DMA((band_count - 1,)), DMA((band_count - 1,))]
    measured, extended, received = communicate(
        functools.partial(begin_kernel, sizes),
        0,
        [SMEM, HBM, HBM, VMEM],
        (
            floats(slot_count, width, width),
            floats(2, tile_rows + width, tile_cols + width),
            jax.ShapeDtypeStruct(wants.shape, jnp.int32),
        ),
        staging + [DMA] + pair_sems + pair_sems + [DMA((3,)), DMA((3,))],
    )(holder, intensities, object_field, wants)
    received = received[:, : 2 * STEPS, :CAP].transpose(1, 0, 2).reshape(2, STEPS, slot_count)
    share_rows = 2 * width // band_count
    summing = [
        pltpu.VMEM((2 * width, width), jnp.float32),
        pltpu.VMEM((band_count - 1, share_rows, width), jnp.float32),
        pltpu.VMEM((strip_count, share_rows, width), jnp.float32),
        DMA((2, band_count - 1)),
        DMA((2, strip_count - 1)),
        DMA((2, band_count - 1)),
    ]
    gradient, probe_term = run_step(received[0, 0], received[1, 0], extended, probe_field, measured, tables)
    measured, extended, probe_field = communicate(
        functools.partial(middle_kernel, sizes, probe_scale),
        1,
        [SMEM, HBM] + [VMEM] * 4,
        (floats(*measured.shape), floats(*extended.shape), floats(*probe_field.shape)),
        staging
        + pair_sems
        + [
            pltpu.VMEM((2, 2, tile_rows + width, width), jnp.float32),
            pltpu.VMEM((2, 2, width, tile_cols + width), jnp.float32),
            pltpu.VMEM((2, 2, width, tile_cols + width), jnp.float32),
        ]
        + [DMA((2,))] * 4
        + summing,
    )(holder, intensities, gradient, probe_term, extended, probe_field)
    gradient, probe_term = run_step(received[0, 1], received[1, 1], extended, probe_field, measured, tables)
    return communicate(
        functools.partial(end_kernel, sizes, probe_scale),
        2,
        [VMEM] * 4,
        (floats(*object_field.shape), floats(*probe_field.shape)),
        [
            pltpu.VMEM((2, tile_rows, width), jnp.float32),
            pltpu.VMEM((2, width, tile_cols), jnp.float32),
            pltpu.VMEM((2, width, width), jnp.float32),
            DMA((3,)),
            DMA((3,)),
        ]
        + summing,
    )(gradient, probe_term, extended, probe_field)


def solution(mesh):
    in_specs = (
        P(None, "ty", "tx"),
        P(),
        P(None, ("ty", "tx"), None),
        P(None, ("ty", "tx")),
        P(None, ("ty", "tx")),
        P(None, ("ty", "tx"), None, None),
    )
    out_specs = (P(None, "ty", "tx"), P())
    return jax.shard_map(
        on_device, mesh=mesh, in_specs=in_specs, out_specs=out_specs, check_vma=False
    )
```

```python
import functools
import math

import jax
import jax.numpy as jnp
import ml_dtypes
import numpy as np
from jax import lax
from jax.experimental import pallas as pl
from jax.experimental.pallas import tpu as pltpu
from jax.sharding import PartitionSpec as P

CAP = 3
STEPS = 2
GROUP = 8
JOINT = 8
ROWS = 8

OBJECT_RATE = 0.25
PROBE_RATE = 1.0


def split_table(table):
    high = table.astype(ml_dtypes.bfloat16)
    low = (table - high.astype(np.float64)).astype(ml_dtypes.bfloat16)
    return high, low


def dft_tables(width):
    counter = np.arange(width)
    radians = (counter[:, None] * counter[None, :] % width) * (2.0 * math.pi / width)
    cos = np.cos(radians) / math.sqrt(width)
    sin = -np.sin(radians) / math.sqrt(width)
    plus = np.block([[cos, -sin], [sin, cos]])
    minus = np.block([[cos, sin], [-sin, cos]])

    def left(table):
        high, low = split_table(table)
        return np.concatenate([high, low, high], axis=1)

    def right(table):
        high, low = split_table(table)
        return np.concatenate([high, low, high], axis=0)

    return np.stack([left(plus), left(minus)]), np.stack([right(minus), right(plus)])


def split(value):
    high = value.astype(jnp.bfloat16)
    low = (value - high.astype(jnp.float32)).astype(jnp.bfloat16)
    return high, low


def left_apply(table, parts):
    data = jnp.concatenate(
        [jnp.concatenate([re for re, _ in parts], axis=1), jnp.concatenate([im for _, im in parts], axis=1)],
        axis=0,
    )
    high, low = split(data)
    out = jnp.dot(table, jnp.concatenate([high, high, low], axis=0), preferred_element_type=jnp.float32)
    width = out.shape[0] // 2
    return [
        (out[:width, i * width : (i + 1) * width], out[width:, i * width : (i + 1) * width])
        for i in range(len(parts))
    ]


def right_apply(table, parts):
    data = jnp.concatenate([jnp.concatenate([re, im], axis=1) for re, im in parts], axis=0)
    high, low = split(data)
    out = jnp.dot(jnp.concatenate([high, high, low], axis=1), table, preferred_element_type=jnp.float32)
    width = out.shape[1] // 2
    return [
        (out[i * width : (i + 1) * width, :width], out[i * width : (i + 1) * width, width:])
        for i in range(len(parts))
    ]


def step_kernel(
    tops, lefts, extended, probe, measured, left_tables, right_tables, gradient, probe_gradient
):
    width = probe.shape[1]
    slots = measured.shape[0]
    gradient[...] = jnp.zeros_like(gradient)
    probe_gradient[...] = jnp.zeros_like(probe_gradient)
    tiles = width // ROWS
    lane = lax.broadcasted_iota(jnp.int32, (tiles + 1, ROWS, width), 2)
    row = lax.broadcasted_iota(jnp.int32, (tiles, ROWS, width), 1)

    def corner(slot):
        top = jnp.maximum(tops[slot], 0)
        left = lefts[slot]
        top_base = pl.multiple_of(top // ROWS * ROWS, ROWS)
        left_base = pl.multiple_of(left // width * width, width)
        return top_base, top - top_base, left_base, left - left_base

    def cut(slot):
        top_base, down, left_base, off = corner(slot)
        rows = pl.ds(top_base, width + ROWS)
        out = []
        for part in range(2):
            near = extended[part, rows, pl.ds(left_base, width)].reshape(lane.shape)
            far = extended[part, rows, pl.ds(left_base + width, width)].reshape(lane.shape)
            value = pltpu.roll(jnp.where(lane < off, far, near), lax.rem(width - off, width), 2)
            value = pltpu.roll(value, lax.rem(ROWS - down, ROWS), 1)
            value = jnp.where(row < ROWS - down, value[:tiles], value[1:])
            out.append(value.reshape(width, width))
        return out

    def add(slot, terms):
        top_base, down, left_base, off = corner(slot)
        rows = pl.ds(top_base, width + ROWS)
        for part in range(2):
            value = pltpu.roll(terms[part].reshape(row.shape), down, 1)
            value = pltpu.roll(value, off, 2)
            upper = jnp.where(row >= down, value, 0.0)
            lower = jnp.where(row >= down, 0.0, value)
            edge = jnp.zeros((1, ROWS, width), jnp.float32)
            value = jnp.concatenate([upper, edge], axis=0) + jnp.concatenate([edge, lower], axis=0)
            near = jnp.where(lane < off, 0.0, value).reshape(width + ROWS, width)
            far = jnp.where(lane < off, value, 0.0).reshape(width + ROWS, width)
            gradient[part, rows, pl.ds(left_base, width)] += near
            gradient[part, rows, pl.ds(left_base + width, width)] += far

    def body(group, carry):
        pairs = [
            [group * GROUP + JOINT * pair + i for i in range(JOINT)] for pair in range(GROUP // JOINT)
        ]
        for pair in pairs:
            patches = [cut(slot) for slot in pair]
            probe_re, probe_im = probe[0], probe[1]
            waves = [
                (probe_re * re - probe_im * im, probe_re * im + probe_im * re) for re, im in patches
            ]
            far = right_apply(right_tables[0], left_apply(left_tables[0], waves))
            scaled = []
            for slot, (re, im) in zip(pair, far):
                filled = jnp.where(tops[slot] >= 0, 1.0, 0.0)
                misfit = (re * re + im * im - measured[slot]) * filled
                scaled.append((misfit * re, misfit * im))
            back = left_apply(left_tables[1], right_apply(right_tables[1], scaled))
            probe_terms = [
                (qr * br + qi * bi, qr * bi - qi * br) for (qr, qi), (br, bi) in zip(patches, back)
            ]
            probe_gradient[:width] += sum(re for re, _ in probe_terms)
            probe_gradient[width:] += sum(im for _, im in probe_terms)
            for slot, (br, bi) in zip(pair, back):
                add(slot, (probe_re * br + probe_im * bi, probe_re * bi - probe_im * br))
        return carry

    lax.fori_loop(0, slots // GROUP, body, 0)


def run_step(tops, lefts, extended, probe, measured, tables):
    vmem = pl.BlockSpec(memory_space=pltpu.VMEM)
    smem = pl.BlockSpec(memory_space=pltpu.SMEM)
    width = probe.shape[1]
    slots = measured.shape[0]
    return pl.pallas_call(
        step_kernel,
        out_shape=(
            jax.ShapeDtypeStruct(extended.shape, jnp.float32),
            jax.ShapeDtypeStruct((2 * width, width), jnp.float32),
        ),
        in_specs=[smem, smem] + [vmem] * 5,
        out_specs=(vmem, vmem),
        compiler_params=pltpu.CompilerParams(vmem_limit_bytes=40 * 1024 * 1024),
        cost_estimate=pl.CostEstimate(
            flops=slots * 24 * 32 * width**3, bytes_accessed=8 * 1024 * 1024, transcendentals=0
        ),
    )(tops, lefts, extended, probe, measured, *tables)


def remote(source, target, send, receive, ty, tx):
    return pltpu.make_async_remote_copy(
        src_ref=source,
        dst_ref=target,
        send_sem=send,
        recv_sem=receive,
        device_id=(ty, tx),
        device_id_type=pl.DeviceIdType.MESH,
    )


def only(condition):
    return pl.when(condition)


def greet(partners):
    barrier = pltpu.get_barrier_semaphore()
    count = 0
    for exists, ty, tx in partners:

        def signal(ty=ty, tx=tx):
            pl.semaphore_signal(
                barrier, inc=1, device_id=(ty, tx), device_id_type=pl.DeviceIdType.MESH
            )

        if exists is True:
            signal()
            count = count + 1
        else:
            only(exists)(signal)
            count = count + exists.astype(jnp.int32)
    pl.semaphore_wait(barrier, count)


def peers(band_count, ty, tx):
    return [(True, lax.rem(ty + k, band_count), tx) for k in range(1, band_count)]


def stage_measured(step_number, intensities, holder, staged, outgoing, measured, load_sem, ty):
    load = pltpu.make_async_copy(intensities.at[step_number], staged, load_sem)
    load.start()
    load.wait()

    def place(slot, carry):
        outgoing[slot] = staged[holder[step_number, slot]]
        return carry

    lax.fori_loop(0, outgoing.shape[0], place, 0)
    for own in range(CAP):
        measured[ty * CAP + own] = staged[holder[step_number, ty * CAP + own]]


def measured_copies(band_count, outgoing, measured, send_sems, recv_sems, ty, tx):
    copies = []
    for k in range(1, band_count):
        peer = lax.rem(ty + k, band_count)
        copies.append(
            remote(
                outgoing.at[pl.ds(peer * CAP, CAP)],
                measured.at[pl.ds(ty * CAP, CAP)],
                send_sems.at[k - 1],
                recv_sems.at[k - 1],
                peer,
                tx,
            )
        )
    return copies


def begin_kernel(
    sizes, holder, intensities, object_field, wants, measured, extended, received,
    staged, outgoing, load_sem, own_sem, send_sems, recv_sems, want_send, want_recv, halo_send, halo_recv,
):
    band_count, strip_count, width = sizes
    ty, tx = lax.axis_index("ty"), lax.axis_index("tx")
    rows, cols = object_field.shape[1:]
    above, left = ty > 0, tx > 0
    below, right = ty < band_count - 1, tx < strip_count - 1
    own = pltpu.make_async_copy(object_field, extended.at[:, :rows, :cols], own_sem)
    own.start()
    greet(
        peers(band_count, ty, tx)
        + [
            (left, ty, tx - 1),
            (right, ty, tx + 1),
            (above & left, ty - 1, tx - 1),
            (below & right, ty + 1, tx + 1),
        ]
    )
    want_copies = []
    for k in range(1, band_count):
        peer = lax.rem(ty + k, band_count)
        want_copies.append(
            remote(wants.at[peer], received.at[ty], want_send.at[k - 1], want_recv.at[k - 1], peer, tx)
        )
    for copy in want_copies:
        copy.start()
    halos = [
        (
            left, right,
            remote(object_field.at[:, :, :width], extended.at[:, :rows, cols:],
                   halo_send.at[0], halo_recv.at[0], ty, tx - 1),
        ),
        (
            above, below,
            remote(object_field.at[:, :width, :], extended.at[:, rows:, :cols],
                   halo_send.at[1], halo_recv.at[1], ty - 1, tx),
        ),
        (
            above & left, below & right,
            remote(object_field.at[:, :width, :width], extended.at[:, rows:, cols:],
                   halo_send.at[2], halo_recv.at[2], ty - 1, tx - 1),
        ),
    ]
    for sends, _, copy in halos:
        only(sends)(copy.start)
    stage_measured(0, intensities, holder, staged, outgoing, measured, load_sem, ty)
    copies = measured_copies(band_count, outgoing, measured, send_sems, recv_sems, ty, tx)
    for copy in copies:
        copy.start()
    received[ty] = wants[ty]

    @only(jnp.logical_not(right))
    def _():
        extended[:, :rows, cols:] = jnp.zeros((2, rows, width), jnp.float32)

    @only(jnp.logical_not(below))
    def _():
        extended[:, rows:, :cols] = jnp.zeros((2, width, cols), jnp.float32)

    @only(jnp.logical_not(below & right))
    def _():
        extended[:, rows:, cols:] = jnp.zeros((2, width, width), jnp.float32)

    own.wait()
    for copy in want_copies:
        copy.wait()
    for sends, receives, copy in halos:
        only(sends)(copy.wait_send)
        only(receives)(copy.wait_recv)
    for copy in copies:
        copy.wait()


def strip_peers(strip_count, ty, tx):
    return [(True, ty, lax.rem(tx + k, strip_count)) for k in range(1, strip_count)]


class ProbeSum:
    def __init__(self, sizes, probe_term, total, band_parts, strip_parts, band_sems, strip_sems, share_sems, ty, tx):
        band_count, strip_count, _ = sizes
        self.ty, self.tx = ty, tx
        self.probe_term, self.total = probe_term, total
        self.band_parts, self.strip_parts = band_parts, strip_parts
        rows = total.shape[0] // band_count
        self.mine = pl.ds(ty * rows, rows)
        self.to_bands, self.to_strips, self.shares = [], [], []
        for k in range(1, band_count):
            peer = lax.rem(ty + k, band_count)
            self.to_bands.append(
                remote(probe_term.at[pl.ds(peer * rows, rows)], band_parts.at[k - 1],
                       band_sems.at[0, k - 1], band_sems.at[1, k - 1], peer, tx)
            )
            self.shares.append(
                remote(total.at[self.mine], total.at[self.mine],
                       share_sems.at[0, k - 1], share_sems.at[1, k - 1], peer, tx)
            )
        for k in range(1, strip_count):
            peer = lax.rem(tx + k, strip_count)
            self.to_strips.append(
                remote(strip_parts.at[tx], strip_parts.at[tx],
                       strip_sems.at[0, k - 1], strip_sems.at[1, k - 1], ty, peer)
            )

    def start(self):
        for copy in self.to_bands:
            copy.start()

    def over_strips(self):
        for copy in self.to_bands:
            copy.wait()
        value = self.probe_term[self.mine, :]
        for k in range(self.band_parts.shape[0]):
            value = value + self.band_parts[k]
        self.strip_parts[self.tx] = value
        for copy in self.to_strips:
            copy.start()

    def share(self):
        for copy in self.to_strips:
            copy.wait()
        value = self.strip_parts[0]
        for k in range(1, self.strip_parts.shape[0]):
            value = value + self.strip_parts[k]
        self.total[self.mine, :] = value
        for copy in self.shares:
            copy.start()

    def finish(self, scale, probe, new_probe):
        for copy in self.shares:
            copy.wait()
        width = probe.shape[1]
        for part in range(2):
            new_probe[part] = probe[part] - scale * self.total[part * width : (part + 1) * width]


def middle_kernel(
    sizes, scale, gradient, probe_term, extended, probe, new_extended, new_probe,
    side, ends, corners, side_send, side_recv, end_send, end_recv, corner_send, corner_recv,
    total, band_parts, strip_parts, band_sems, strip_sems, share_sems,
):
    band_count, strip_count, width = sizes
    ty, tx = lax.axis_index("ty"), lax.axis_index("tx")
    rows, cols = (size - width for size in extended.shape[1:])
    above, left = ty > 0, tx > 0
    below, right = ty < band_count - 1, tx < strip_count - 1
    diagonals = [
        (below & right, above & left, 1, 1),
        (below & left, above & right, 1, -1),
        (above & right, below & left, -1, 1),
        (above & left, below & right, -1, -1),
    ]
    greet(
        peers(band_count, ty, tx)
        + strip_peers(strip_count, ty, tx)
        + [(sends, ty + down, tx + across) for sends, _, down, across in diagonals]
    )
    probe_sum = ProbeSum(
        sizes, probe_term, total, band_parts, strip_parts, band_sems, strip_sems, share_sems, ty, tx
    )
    probe_sum.start()
    sides = [
        (right, left, remote(gradient.at[:, :, cols:], side.at[0], side_send.at[0], side_recv.at[0], ty, tx + 1)),
        (left, right, remote(gradient.at[:, :, :width], side.at[1], side_send.at[1], side_recv.at[1], ty, tx - 1)),
    ]
    end_copies = [
        (below, above, remote(gradient.at[:, rows:, :], ends.at[0], end_send.at[0], end_recv.at[0], ty + 1, tx)),
        (above, below, remote(gradient.at[:, :width, :], ends.at[1], end_send.at[1], end_recv.at[1], ty - 1, tx)),
    ]
    corner_copies = []
    for number, (sends, receives, down, across) in enumerate(diagonals):
        block = gradient.at[:, pl.ds(rows if down > 0 else 0, width), pl.ds(cols if across > 0 else 0, width)]
        corner_copies.append(
            (
                sends, receives,
                remote(block, corners.at[number], corner_send.at[number], corner_recv.at[number],
                       ty + down, tx + across),
            )
        )
    bulk = sides + end_copies + corner_copies
    targets = [side.at[0], side.at[1], ends.at[0], ends.at[1]] + [corners.at[number] for number in range(4)]
    probe_sum.over_strips()
    for sends, _, copy in bulk:
        only(sends)(copy.start)
    probe_sum.share()
    for (_, receives, _), target in zip(bulk, targets):

        @only(jnp.logical_not(receives))
        def _(target=target):
            target[...] = jnp.zeros(target.shape, jnp.float32)

    inner = slice(width, rows)
    middle = slice(width, cols)
    new_extended[:, inner, middle] = extended[:, inner, middle] - OBJECT_RATE * gradient[:, inner, middle]
    for sends, receives, copy in bulk:
        only(sends)(copy.wait_send)
        only(receives)(copy.wait_recv)
    first, last = slice(0, width), slice(cols, cols + width)
    for number, lanes in enumerate((first, last)):
        new_extended[:, inner, lanes] = extended[:, inner, lanes] - OBJECT_RATE * (
            gradient[:, inner, lanes] + side[number, :, inner, :]
        )
    for number, block in enumerate((slice(0, width), slice(rows, rows + width))):
        new_extended[:, block, middle] = extended[:, block, middle] - OBJECT_RATE * (
            gradient[:, block, middle] + ends[number, :, :, middle]
        )
        for edge, lanes in enumerate((first, last)):
            new_extended[:, block, lanes] = extended[:, block, lanes] - OBJECT_RATE * (
                gradient[:, block, lanes]
                + ends[number, :, :, lanes]
                + side[edge, :, block, :]
                + corners[2 * number + edge]
            )
    probe_sum.finish(scale, probe, new_probe)


def end_kernel(
    sizes, scale, gradient, probe_term, extended, probe, new_object, new_probe,
    side, end, corner, halo_send, halo_recv,
    total, band_parts, strip_parts, band_sems, strip_sems, share_sems,
):
    band_count, strip_count, width = sizes
    ty, tx = lax.axis_index("ty"), lax.axis_index("tx")
    rows, cols = new_object.shape[1:]
    above, left = ty > 0, tx > 0
    below, right = ty < band_count - 1, tx < strip_count - 1
    greet(
        peers(band_count, ty, tx)
        + strip_peers(strip_count, ty, tx)
        + [(above & left, ty - 1, tx - 1), (below & right, ty + 1, tx + 1)]
    )
    probe_sum = ProbeSum(
        sizes, probe_term, total, band_parts, strip_parts, band_sems, strip_sems, share_sems, ty, tx
    )
    probe_sum.start()
    halos = [
        (right, left, side, remote(gradient.at[:, :rows, cols:], side, halo_send.at[0], halo_recv.at[0], ty, tx + 1)),
        (below, above, end, remote(gradient.at[:, rows:, :cols], end, halo_send.at[1], halo_recv.at[1], ty + 1, tx)),
        (
            below & right, above & left, corner,
            remote(gradient.at[:, rows:, cols:], corner, halo_send.at[2], halo_recv.at[2], ty + 1, tx + 1),
        ),
    ]
    only(halos[1][0])(halos[1][3].start)
    probe_sum.over_strips()
    only(halos[0][0])(halos[0][3].start)
    only(halos[2][0])(halos[2][3].start)
    probe_sum.share()
    for _, receives, target, _ in halos:

        @only(jnp.logical_not(receives))
        def _(target=target):
            target[...] = jnp.zeros(target.shape, jnp.float32)

    new_object[:, width:, width:] = (
        extended[:, width:rows, width:cols] - OBJECT_RATE * gradient[:, width:rows, width:cols]
    )
    probe_sum.finish(scale, probe, new_probe)
    for sends, receives, _, copy in halos:
        only(sends)(copy.wait_send)
        only(receives)(copy.wait_recv)
    new_object[:, width:, :width] = extended[:, width:rows, :width] - OBJECT_RATE * (
        gradient[:, width:rows, :width] + side[:, width:, :]
    )
    new_object[:, :width, width:] = extended[:, :width, width:cols] - OBJECT_RATE * (
        gradient[:, :width, width:cols] + end[:, :, width:]
    )
    new_object[:, :width, :width] = extended[:, :width, :width] - OBJECT_RATE * (
        gradient[:, :width, :width] + side[:, :width, :] + end[:, :, :width] + corner[...]
    )


VMEM = pl.BlockSpec(memory_space=pltpu.VMEM)
SMEM = pl.BlockSpec(memory_space=pltpu.SMEM)
HBM = pl.BlockSpec(memory_space=pl.ANY)
DMA = pltpu.SemaphoreType.DMA


def floats(*shape):
    return jax.ShapeDtypeStruct(shape, jnp.float32)


def communicate(kernel, number, in_specs, shapes, scratch):
    return pl.pallas_call(
        kernel,
        out_shape=shapes,
        in_specs=in_specs,
        out_specs=tuple(VMEM for _ in shapes),
        scratch_shapes=scratch,
        compiler_params=pltpu.CompilerParams(
            collective_id=number, has_side_effects=True, vmem_limit_bytes=48 * 1024 * 1024
        ),
    )


def on_device(object_field, probe_field, owners, row_offsets, col_offsets, intensities):
    band_count = lax.axis_size("ty")
    strip_count = lax.axis_size("tx")
    tile_rows = object_field.shape[1]
    tile_cols = object_field.shape[2]
    width = probe_field.shape[1]
    batch_rows = row_offsets.shape[1]
    slot_count = band_count * CAP
    strip_index = lax.axis_index("tx")
    tables = [jnp.asarray(table) for table in dft_tables(width)]
    probe_scale = PROBE_RATE / (batch_rows * band_count * strip_count)

    owner_rows = owners[:, :, 0]
    position_ids = jnp.arange(batch_rows, dtype=jnp.int32)
    earlier = (owner_rows[:, None, :] == owner_rows[:, :, None]) & (
        position_ids[None, None, :] < position_ids[None, :, None]
    )
    slot_of = owner_rows * CAP + jnp.sum(earlier.astype(jnp.int32), axis=2)
    top_local = (
        jnp.minimum(owner_rows * tile_rows + row_offsets, tile_rows * band_count - width)
        - owner_rows * tile_rows
    )
    left_local = (
        jnp.minimum(strip_index * tile_cols + col_offsets, tile_cols * strip_count - width)
        - strip_index * tile_cols
    )
    slot_ids = jnp.arange(slot_count, dtype=jnp.int32)
    matches = slot_of[:, None, :] == slot_ids[None, :, None]
    filled = jnp.any(matches, axis=2)

    def by_slot(values):
        return jnp.sum(jnp.where(matches, values[:, None, :], 0), axis=2)

    want_top = jnp.where(filled, by_slot(top_local), -1)
    want_left = by_slot(left_local)
    holder = by_slot(jnp.broadcast_to(position_ids[None], slot_of.shape))
    sizes = (band_count, strip_count, width)
    wants = jnp.concatenate([want_top, want_left]).reshape(2 * STEPS, band_count, CAP).transpose(1, 0, 2)
    wants = jnp.pad(wants, ((0, 0), (0, 8 - 2 * STEPS), (0, 128 - CAP)))
    staging = [
        pltpu.VMEM((batch_rows, width, width), jnp.float32),
        pltpu.VMEM((slot_count, width, width), jnp.float32),
        DMA,
    ]
    pair_sems = [DMA((band_count - 1,)), DMA((band_count - 1,))]
    measured, extended, received = communicate(
        functools.partial(begin_kernel, sizes),
        0,
        [SMEM, HBM, HBM, VMEM],
        (
            floats(slot_count, width, width),
            floats(2, tile_rows + width, tile_cols + width),
            jax.ShapeDtypeStruct(wants.shape, jnp.int32),
        ),
        staging + [DMA] + pair_sems + pair_sems + [DMA((3,)), DMA((3,))],
    )(holder, intensities, object_field, wants)
    received = received[:, : 2 * STEPS, :CAP].transpose(1, 0, 2).reshape(2, STEPS, slot_count)
    share_rows = 2 * width // band_count
    summing = [
        pltpu.VMEM((2 * width, width), jnp.float32),
        pltpu.VMEM((band_count - 1, share_rows, width), jnp.float32),
        pltpu.VMEM((strip_count, share_rows, width), jnp.float32),
        DMA((2, band_count - 1)),
        DMA((2, strip_count - 1)),
        DMA((2, band_count - 1)),
    ]
    later, _ = lax.optimization_barrier(
        (
            jnp.take(intensities.reshape(-1, width, width), holder[1] + batch_rows, axis=0, mode="clip"),
            received,
        )
    )
    later = lax.all_to_all(
        later.reshape(band_count, CAP, width, width), "ty", split_axis=0, concat_axis=0, tiled=True
    ).reshape(slot_count, width, width)
    gradient, probe_term = run_step(received[0, 0], received[1, 0], extended, probe_field, measured, tables)
    extended, probe_field = communicate(
        functools.partial(middle_kernel, sizes, probe_scale),
        1,
        [VMEM] * 4,
        (floats(*extended.shape), floats(*probe_field.shape)),
        [
            pltpu.VMEM((2, 2, tile_rows + width, width), jnp.float32),
            pltpu.VMEM((2, 2, width, tile_cols + width), jnp.float32),
            pltpu.VMEM((4, 2, width, width), jnp.float32),
        ]
        + [DMA((2,))] * 4
        + [DMA((4,))] * 2
        + summing,
    )(gradient, probe_term, extended, probe_field)
    gradient, probe_term = run_step(received[0, 1], received[1, 1], extended, probe_field, later, tables)
    return communicate(
        functools.partial(end_kernel, sizes, probe_scale),
        2,
        [VMEM] * 4,
        (floats(*object_field.shape), floats(*probe_field.shape)),
        [
            pltpu.VMEM((2, tile_rows, width), jnp.float32),
            pltpu.VMEM((2, width, tile_cols), jnp.float32),
            pltpu.VMEM((2, width, width), jnp.float32),
            DMA((3,)),
            DMA((3,)),
        ]
        + summing,
    )(gradient, probe_term, extended, probe_field)


def solution(mesh):
    in_specs = (
        P(None, "ty", "tx"),
        P(),
        P(None, ("ty", "tx"), None),
        P(None, ("ty", "tx")),
        P(None, ("ty", "tx")),
        P(None, ("ty", "tx"), None, None),
    )
    out_specs = (P(None, "ty", "tx"), P())
    return jax.shard_map(
        on_device, mesh=mesh, in_specs=in_specs, out_specs=out_specs, check_vma=False
    )
```
